512 devices in a mesh: seq: 64 (over z, x, core), head: 8 (over y).
Axes of the slice: x: 4, y: 8, z: 8, core: 2. Of those that a mesh axis runs over, the one named last changes fastest.
Arguments:
- queries: bfloat16 [16384, 2048], P('seq', 'head'), may hold values from -6 to 6
- key_rows: bfloat16 [16384, 2048], P('seq', 'head'), may hold values from -6 to 6
- value_rows: bfloat16 [16384, 4096], P('seq', 'head'), may hold values from -6 to 6
- input_gate: float32 [8, 16384], P('head', 'seq'), may hold values from -6 to 260
- forget_gate: float32 [8, 16384], P('head', 'seq'), as said below
- norm_gain: float32 [4096], P('head'), may hold values from 0.1 to 1.9
- output_gate: bfloat16 [16384, 4096], P('seq', 'head'), may hold values from -6 to 6
- out_weight: bfloat16 [4096, 4096], P('head', 'seq'), may hold values from -0.25 to 0.25
Outputs:
- layer_out: bfloat16 [16384, 4096], P('seq', 'head')
The draws below stay inside these ranges and needn't reach their ends.
Inputs may be any that keep to these rules, and one draw needn't show every extreme that they name: `forget_gate`: forget-gate preactivations.
All inputs are finite; a program needn't handle non-finite values.
Results may differ from the reference program's by a relative error of at most 0.017.
Values may be sent and summed in bfloat16 or wider, within the bound.
No kernel may reach another device: no remote copies, remote signals or barrier semaphores. Data moves between devices by JAX's collectives and lax.ppermute only.
A program may use at most 128 MiB of HBM per device.

```python
import jax
import jax.numpy as jnp
from jax import lax

D = 4096
DK = 256
DV = 512
TOK_DEV = 256
HEAD_COUNT = 8
TOKENS = 16384


def draw_input_gate(key, part):
    key = jax.random.fold_in(key, 11)
    first = jax.random.fold_in(key, 0)
    value_matrix = jax.random.uniform(first, (HEAD_COUNT, TOKENS), jnp.float32, -6.0, 6.0)
    return value_matrix


def draw_forget_gate(key, part):
    key = jax.random.fold_in(key, 23)
    key_matrix = jax.random.split(key, 6)
    slow_share = 0.5
    slow = jax.random.bernoulli(key_matrix[0], slow_share, (HEAD_COUNT, 1))
    slow_level = jnp.log(TOKENS / jax.random.uniform(key_matrix[1], (HEAD_COUNT, 1), jnp.float32, 0.25, 1.0))
    fast_level = jnp.log(40.0 * jax.random.uniform(key_matrix[2], (HEAD_COUNT, 1), jnp.float32, 0.75, 1.25))
    noise = jax.random.uniform(key_matrix[3], (HEAD_COUNT, TOKENS), jnp.float32, -0.7, 0.7)
    value_matrix = jnp.where(slow, slow_level, fast_level) + noise
    token_positions = jax.random.randint(key_matrix[4], (HEAD_COUNT, 2), 0, TOKENS)
    segment_groups = jax.random.uniform(key_matrix[5], (HEAD_COUNT, 2), jnp.float32, 0.0, 1.39)
    rows_per_head = jnp.broadcast_to(jnp.arange(HEAD_COUNT)[:, None], (HEAD_COUNT, 2))
    return value_matrix.at[rows_per_head, token_positions].set(segment_groups)


def spiked(values, key, source, target, parts, factor):
    def block_of(position):
        return (jnp.arange(values.shape[position]) // (values.shape[position] // parts)).reshape((-1,) + (1,) * (values.ndim - 1 - position))

    one_side = jax.random.permutation(key, parts)[block_of(target)]
    other_side = (block_of(target) + parts // 2) % parts
    return jnp.where((block_of(source) == one_side) | (block_of(source) == other_side), factor * values, values)


def steps_of(key, extent, pieces, smallest, top_value):
    def one(dim, parts):
        heights = jax.random.uniform(jax.random.fold_in(jax.random.fold_in(key, 6), dim), (parts,), jnp.float32, smallest / len(pieces), top_value / len(pieces))
        return jnp.repeat(jnp.exp(heights), extent[dim] // parts).reshape((-1,) + (1,) * (len(extent) - dim - 1))

    loudness = one(*pieces[0])
    for cut in pieces[1:]:
        loudness = loudness * one(*cut)
    return loudness


def normal_values(key, shape, scale, limit, cuts=(), dtype=jnp.bfloat16):
    entries = scale * jax.random.normal(key, shape, jnp.float32)
    if cuts:
        entries = entries * steps_of(key, shape, cuts, -0.22, 0.18)
    return jnp.clip(entries, -limit, limit).astype(dtype)


def heavy_noise(own_key, dims, deviation, bound, cuts, heavy, held_as=jnp.bfloat16):
    entries = deviation * jax.random.normal(own_key, dims, jnp.float32)
    if cuts:
        entries = entries * steps_of(own_key, dims, cuts, -0.22, 0.18)
    return jnp.clip(spiked(entries, jax.random.fold_in(own_key, 3), *heavy), -bound, bound).astype(held_as)


def setup_inputs(seed: int = 0) -> dict:
    arg_keys = jax.random.split(jax.random.key(seed), 9)
    queries = normal_values(arg_keys[0], (TOKENS, HEAD_COUNT * DK), 1.0, 6.0, ((0, 64), (1, 8)))
    key_rows = normal_values(arg_keys[1], (TOKENS, HEAD_COUNT * DK), 1.0, 6.0, ((0, 64), (1, 8)))
    value_rows = normal_values(arg_keys[2], (TOKENS, HEAD_COUNT * DV), 1.0, 6.0, ((0, 64), (1, 8)))
    input_gate = draw_input_gate(jax.random.fold_in(arg_keys[8], 71), 0)
    forget_gate = draw_forget_gate(jax.random.fold_in(arg_keys[8], 71), 0)
    norm_gain = jnp.clip(1.0 + 0.18 * jax.random.normal(arg_keys[5], (HEAD_COUNT * DV,), jnp.float32), 0.1, 1.9)
    output_gate = normal_values(arg_keys[6], (TOKENS, HEAD_COUNT * DV), 1.0, 6.0, ((0, 64), (1, 8)))
    out_weight = heavy_noise(arg_keys[7], (HEAD_COUNT * DV, D), (HEAD_COUNT * DV) ** -0.5, 0.25, ((0, 8), (1, 64)), (0, 1, 64, 4.0))
    return dict(queries=queries, key_rows=key_rows, value_rows=value_rows, input_gate=input_gate, forget_gate=forget_gate, norm_gain=norm_gain, output_gate=output_gate, out_weight=out_weight)


NEG = -1e+30

def block_step(carry, block):
    state, prev_max = carry
    query_blk, key_blk, value_blk, gate_in, gate_forget = block
    inv_root = 1.0 / DK ** 0.5
    cum_forget = jnp.cumsum(jax.nn.log_sigmoid(gate_forget))
    places = jnp.arange(TOK_DEV)
    causal = places[:, None] >= places[None, :]
    log_weight = jnp.where(causal, cum_forget[:, None] - cum_forget[None, :] + gate_in[None, :], NEG)
    row_max = jnp.maximum(cum_forget + prev_max, lax.optimization_barrier(jnp.max(log_weight, axis=1)))
    scores = jnp.dot(query_blk, key_blk.T, preferred_element_type=jnp.float32) * inv_root
    weights = (jnp.exp(log_weight - row_max[:, None]) * scores).astype(jnp.bfloat16)
    intra = jnp.dot(weights, value_blk, preferred_element_type=jnp.float32)
    carried = jnp.dot(query_blk, state.astype(jnp.bfloat16), preferred_element_type=jnp.float32) * inv_root
    memory = intra + jnp.exp(cum_forget + prev_max - row_max)[:, None] * carried
    decay = cum_forget[-1]
    end_weight = decay - cum_forget + gate_in
    end_max = jnp.max(end_weight)
    scaled_keys = (key_blk.astype(jnp.float32) * jnp.exp(end_weight - end_max)[:, None]).astype(jnp.bfloat16)
    local_state = jnp.dot(scaled_keys.T, value_blk, preferred_element_type=jnp.float32)
    new_max = jnp.maximum(decay + prev_max, end_max)
    new_state = jnp.exp(decay + prev_max - new_max) * state + jnp.exp(end_max - new_max) * local_state
    return ((new_state, new_max), memory)

def head_memory(query_head, key_head, value_head, gate_in, gate_forget):
    blocks = TOKENS // TOK_DEV
    inputs = (query_head.reshape(blocks, TOK_DEV, DK), key_head.reshape(blocks, TOK_DEV, DK), value_head.reshape(blocks, TOK_DEV, DV), gate_in.reshape(blocks, TOK_DEV), gate_forget.reshape(blocks, TOK_DEV))
    start = (jnp.zeros((DK, DV), jnp.float32), jnp.asarray(NEG, jnp.float32))
    unused_carry, rows = lax.scan(block_step, start, inputs)
    return rows.reshape(TOKENS, DV)

def reference(queries, key_rows, value_rows, input_gate, forget_gate, norm_gain, output_gate, out_weight):

    def add_head(index, total):
        key_offset = (index * DK).astype(jnp.int32)
        value_offset = (index * DV).astype(jnp.int32)
        head_at = index.astype(jnp.int32)
        memory = head_memory(lax.dynamic_slice_in_dim(queries, key_offset, DK, 1), lax.dynamic_slice_in_dim(key_rows, key_offset, DK, 1), lax.dynamic_slice_in_dim(value_rows, value_offset, DV, 1), lax.dynamic_index_in_dim(input_gate, head_at, 0, keepdims=False), lax.dynamic_index_in_dim(forget_gate, head_at, 0, keepdims=False))
        centred = memory - lax.optimization_barrier(jnp.mean(memory, axis=1, keepdims=True))
        spread = lax.optimization_barrier(jnp.mean(centred * centred, axis=1, keepdims=True))
        gain_head = lax.dynamic_slice_in_dim(norm_gain, value_offset, DV, 0)
        gate_out = jax.nn.sigmoid(lax.dynamic_slice_in_dim(output_gate, value_offset, DV, 1).astype(jnp.float32))
        normed = (centred * lax.rsqrt(spread + 1e-06) * gain_head * gate_out).astype(jnp.bfloat16)
        weight_rows = lax.dynamic_slice_in_dim(out_weight, value_offset, DV, 0)
        partial_value = jnp.dot(normed, weight_rows, preferred_element_type=jnp.float32).astype(jnp.bfloat16)
        partial_value = lax.optimization_barrier(partial_value)
        return total + partial_value.astype(jnp.float32)
    total = lax.fori_loop(0, HEAD_COUNT, add_head, jnp.zeros((TOKENS, D), jnp.float32))
    return total.astype(jnp.bfloat16)
```

```python
import functools
import math

import jax
import jax.numpy as jnp
from jax import lax
from jax.experimental import pallas as pl
from jax.experimental.pallas import tpu as pltpu
from jax.sharding import Mesh, PartitionSpec as P

NEG = -1e30
TILE = (16, 128)
F32 = jnp.float32
BF16 = jnp.bfloat16
VMEM = pl.BlockSpec(memory_space=pltpu.VMEM)
SMEM = pl.BlockSpec(memory_space=pltpu.SMEM)


def call(kernel, out_shape, n_scalar, n_vector, scratch=(), flops=0, vmem=48):
    return pl.pallas_call(
        kernel,
        out_shape=out_shape,
        in_specs=[SMEM] * n_scalar + [VMEM] * n_vector,
        out_specs=jax.tree.map(lambda _: VMEM, out_shape),
        scratch_shapes=list(scratch),
        compiler_params=pltpu.CompilerParams(vmem_limit_bytes=vmem * 2**20),
        cost_estimate=pl.CostEstimate(flops=flops, bytes_accessed=2**20, transcendentals=0),
    )


def tiles(rows, cols):
    return [(r, c) for r in range(0, rows, TILE[0]) for c in range(0, cols, TILE[1])]


def split3(value):
    high = value.astype(BF16).astype(F32)
    middle = (value - high).astype(BF16).astype(F32)
    return high, middle, value - high - middle


def scalar_tile(end_max, decay):
    rows = lax.broadcasted_iota(jnp.int32, TILE, 0)
    held = jnp.zeros(TILE, F32)
    for place, term in enumerate(split3(end_max) + split3(decay)):
        held = jnp.where(rows == place, jnp.broadcast_to(term, TILE), held)
    return held.astype(BF16)


def scalars_of(tile):
    held = tile.astype(F32)
    end_max = held[0:1] + held[1:2] + held[2:3]
    decay = held[3:4] + held[4:5] + held[5:6]
    return end_max, decay


def front_kernel(key_ref, value_ref, in_ref, forget_ref, tiles_ref, cum_ref):
    length = key_ref.shape[0]
    gate = forget_ref[...]
    log_forget = jnp.minimum(gate, 0.0) - jnp.log1p(jnp.exp(-jnp.abs(gate)))
    log_forget = jnp.broadcast_to(log_forget, (8, length))
    before = lax.broadcasted_iota(jnp.int32, (length, length), 0)
    after = lax.broadcasted_iota(jnp.int32, (length, length), 1)
    upper = jnp.where(before <= after, 1.0, 0.0).astype(F32)
    cum = jnp.dot(log_forget, upper, precision=lax.Precision.HIGHEST, preferred_element_type=F32)
    cum_ref[...] = cum
    decay = cum[0:1, length - 1 : length]
    end_weight = decay - cum[0:1] + in_ref[...]
    end_max = jnp.max(end_weight, axis=1, keepdims=True)
    scaled = (key_ref[...].astype(F32).T * jnp.exp(end_weight - end_max)).astype(BF16)
    state = jnp.dot(scaled, value_ref[...], preferred_element_type=F32).astype(BF16)
    places = tiles(*state.shape)
    for place, (row, col) in enumerate(places):
        tiles_ref[place] = state[row : row + TILE[0], col : col + TILE[1]]
    tiles_ref[len(places)] = scalar_tile(end_max, decay)


def pair_kernel(core_ref, both_ref, send_ref):
    core = core_ref[0]
    owners = send_ref.shape[0]
    last = both_ref.shape[1] - 1
    half = last // 2
    per = half // owners
    max_0, decay_0 = scalars_of(both_ref[0, last])
    max_1, decay_1 = scalars_of(both_ref[1, last])
    end_max = jnp.maximum(decay_1 + max_0, max_1)
    scale_0 = jnp.exp(decay_1 + max_0 - end_max)
    scale_1 = jnp.exp(max_1 - end_max)
    scalars = scalar_tile(end_max, decay_0 + decay_1)
    for owner in range(owners):
        for piece in range(per):
            place = core * half + owner * per + piece
            send_ref[owner, piece * 16 : piece * 16 + 16] = (
                scale_0 * both_ref[0, place].astype(F32) + scale_1 * both_ref[1, place].astype(F32)
            ).astype(BF16)
        send_ref[owner, per * 16 : per * 16 + 16] = scalars


def prefix_kernel(chip_ref, held_ref, state_ref, max_ref, maxes):
    chips, rows, lanes = state_ref.shape
    state = jnp.zeros((rows, lanes), F32)
    start_max = jnp.full((1, lanes), NEG, F32)
    for chip in range(chips):
        state_ref[chip] = state.astype(BF16)
        maxes[chip] = jnp.broadcast_to(start_max, (8, lanes))
        end_max, decay = scalars_of(held_ref[chip, rows : rows + 16])
        new_max = jnp.maximum(decay + start_max, end_max)
        state = jnp.exp(decay + start_max - new_max) * state + jnp.exp(
            end_max - new_max
        ) * held_ref[chip, 0:rows].astype(F32)
        start_max = new_max
    max_ref[...] = maxes[chip_ref[0]]


def memory_kernel(
    core_ref, query_ref, key_ref, value_ref, in_ref, cum_ref, gain_ref, gate_ref,
    tiles_ref, both_ref, max_ref, normed_ref, state
):
    length, width = query_ref.shape
    inv_root = 1.0 / math.sqrt(width)
    second = core_ref[0] == 1
    chip_max = max_ref[0:1]
    first_max, first_decay = scalars_of(both_ref[0, both_ref.shape[1] - 1])
    moved = jnp.maximum(first_decay + chip_max, first_max)
    start = jnp.where(second, moved, chip_max)
    keep = jnp.where(second, jnp.exp(first_decay + chip_max - moved), 1.0)
    add = jnp.where(second, jnp.exp(first_max - moved), 0.0)
    for place, (row, col) in enumerate(tiles(*state.shape)):
        state[row : row + TILE[0], col : col + TILE[1]] = (
            keep * tiles_ref[place].astype(F32) + add * both_ref[0, place].astype(F32)
        ).astype(BF16)
    start_max = start[:, 0:1]
    cum_row = cum_ref[0:1]
    cum_col = cum_ref[...].T[:, 0:1]
    at = lax.broadcasted_iota(jnp.int32, (length, length), 0)
    by = lax.broadcasted_iota(jnp.int32, (length, length), 1)
    log_weight = jnp.where(at >= by, cum_col - cum_row + in_ref[...], NEG)
    carried_weight = cum_col + start_max
    row_max = jnp.maximum(carried_weight, jnp.max(log_weight, axis=1, keepdims=True))
    scores = (
        lax.dot_general(
            query_ref[...], key_ref[...], (((1,), (1,)), ((), ())), preferred_element_type=F32
        )
        * inv_root
    )
    weights = (jnp.exp(log_weight - row_max) * scores).astype(BF16)
    intra = jnp.dot(weights, value_ref[...], preferred_element_type=F32)
    carried = jnp.dot(query_ref[...], state[...], preferred_element_type=F32) * inv_root
    memory = intra + jnp.exp(carried_weight - row_max) * carried
    centred = memory - jnp.mean(memory, axis=1, keepdims=True)
    spread = jnp.mean(centred * centred, axis=1, keepdims=True)
    gate_out = jax.nn.sigmoid(gate_ref[...].astype(F32))
    normed_ref[...] = (
        centred * lax.rsqrt(spread + 1e-06) * gain_ref[...] * gate_out
    ).astype(BF16)


def project_kernel(heads, slot_ref, *refs):
    normed, weight_ref, out_ref = refs[:heads], refs[heads], refs[heads + 1]
    width = normed[0].shape[1]
    total = jnp.zeros(out_ref.shape, F32)
    for place in range(heads):
        rows = weight_ref[slot_ref[place]].reshape(out_ref.shape[1], width)
        total += lax.dot_general(
            normed[place][...], rows, (((1,), (1,)), ((), ())), preferred_element_type=F32
        )
    out_ref[...] = total.astype(BF16)


def ring_gather(block, axis, size):
    up = [(i, (i + 1) % size) for i in range(size)]
    down = [(i, (i - 1) % size) for i in range(size)]
    gathered = [(0, block)]
    right = left = block
    for step in range(1, (size + 1) // 2):
        right = lax.ppermute(right, axis, up)
        left = lax.ppermute(left, axis, down)
        gathered += [(-step, right), (step, left)]
    half = block.shape[0] // 2
    right = lax.ppermute(right[:half], axis, up)
    left = lax.ppermute(left[half:], axis, down)
    gathered.append((size // 2, jnp.concatenate([right, left], axis=0)))
    return gathered


def local(sizes, queries, key_rows, value_rows, input_gate, forget_gate, norm_gain, output_gate, out_weight):
    planes, columns, cores, heads = sizes
    chips = planes * columns
    length, key_width = queries.shape
    value_width = value_rows.shape[1]
    core = lax.axis_index("c")
    head = lax.axis_index("y")
    chip = lax.axis_index(("z", "x"))
    count = key_width * value_width // (TILE[0] * TILE[1])
    per = count // 2 // chips

    swap = [
        (z * heads + h, ((h + heads // 2) % heads) * heads + z)
        for z in range(planes)
        for h in range(heads)
    ]
    weight = lax.ppermute(out_weight.T, ("z", "y"), swap)
    weight = lax.all_gather(weight, ("z", "x", "c"))
    weight = weight.reshape(planes, columns * cores, *weight.shape[-2:])

    state_tiles, cum = call(
        front_kernel,
        (
            jax.ShapeDtypeStruct((count + 1, *TILE), BF16),
            jax.ShapeDtypeStruct((8, length), F32),
        ),
        0,
        4,
    )(key_rows, value_rows, input_gate, forget_gate)
    both = lax.all_gather(state_tiles, "c")
    send = call(
        pair_kernel, jax.ShapeDtypeStruct((chips, (per + 1) * TILE[0], TILE[1]), BF16), 1, 1
    )(core[None], both)
    held = lax.all_to_all(send, ("z", "x"), 0, 0, tiled=True)
    starts, start_max = call(
        prefix_kernel,
        (
            jax.ShapeDtypeStruct((chips, per * TILE[0], TILE[1]), BF16),
            jax.ShapeDtypeStruct((8, TILE[1]), F32),
        ),
        1,
        1,
        [pltpu.VMEM((chips, 8, TILE[1]), F32)],
    )(chip[None], held)
    back = lax.all_to_all(starts, ("z", "x"), 0, 0, tiled=True)
    start_tiles = lax.all_gather(back, "c").reshape(count, *TILE)
    normed = call(
        memory_kernel,
        jax.ShapeDtypeStruct((length, value_width), BF16),
        1,
        10,
        [pltpu.VMEM((key_width, value_width), BF16)],
    )(
        core[None], queries, key_rows, value_rows, input_gate, cum, norm_gain[None],
        output_gate, start_tiles, both, start_max
    )
    gathered = ring_gather(normed, "y", heads)
    slots = jnp.stack([(head + place + heads // 2) % heads for place, _ in gathered])
    return call(
        functools.partial(project_kernel, heads),
        jax.ShapeDtypeStruct((length, value_width), BF16),
        1,
        heads + 1,
        flops=2 * length * value_width * value_width * heads,
    )(slots.astype(jnp.int32), *[block for _, block in gathered], weight)


def solution(mesh, sizes=(8, 4, 2, 8)):
    grid = Mesh(mesh.devices.reshape(sizes), ("z", "x", "c", "y"))
    seq = ("z", "x", "c")
    in_specs = (
        P(seq, "y"), P(seq, "y"), P(seq, "y"), P("y", seq), P("y", seq), P("y"), P(seq, "y"), P("y", seq)
    )
    return jax.shard_map(
        functools.partial(local, sizes), mesh=grid, in_specs=in_specs, out_specs=P(seq, "y"), check_vma=False
    )
```

```python
import functools
import math

import jax
import jax.numpy as jnp
from jax import lax
from jax.experimental import pallas as pl
from jax.experimental.pallas import tpu as pltpu
from jax.sharding import Mesh, PartitionSpec as P

NEG = -1e30
TILE = (16, 128)
F32 = jnp.float32
BF16 = jnp.bfloat16
VMEM = pl.BlockSpec(memory_space=pltpu.VMEM)
SMEM = pl.BlockSpec(memory_space=pltpu.SMEM)
HBM = pl.BlockSpec(memory_space=pl.ANY)


def call(kernel, out_shape, places, scratch=(), flops=0, moved=2**20, vmem=48):
    return pl.pallas_call(
        kernel,
        out_shape=out_shape,
        in_specs=[{"s": SMEM, "v": VMEM, "h": HBM}[place] for place in places],
        out_specs=jax.tree.map(lambda _: VMEM, out_shape),
        scratch_shapes=list(scratch),
        compiler_params=pltpu.CompilerParams(vmem_limit_bytes=vmem * 2**20),
        cost_estimate=pl.CostEstimate(flops=flops, bytes_accessed=moved, transcendentals=0),
    )


def fetch(refs, held, semaphores):
    copies = [
        pltpu.make_async_copy(ref, buffer, semaphores.at[place])
        for place, (ref, buffer) in enumerate(zip(refs, held))
    ]
    for copy in copies:
        copy.start()
    return copies


def tiles(rows, cols):
    return [(r, c) for r in range(0, rows, TILE[0]) for c in range(0, cols, TILE[1])]


def split3(value):
    high = value.astype(BF16).astype(F32)
    middle = (value - high).astype(BF16).astype(F32)
    return high, middle, value - high - middle


def scalar_tile(end_max, decay):
    rows = lax.broadcasted_iota(jnp.int32, TILE, 0)
    held = jnp.zeros(TILE, F32)
    for place, term in enumerate(split3(end_max) + split3(decay)):
        held = jnp.where(rows == place, jnp.broadcast_to(term, TILE), held)
    return held.astype(BF16)


def scalars_of(tile):
    held = tile.astype(F32)
    end_max = held[0:1] + held[1:2] + held[2:3]
    decay = held[3:4] + held[4:5] + held[5:6]
    return end_max, decay


def front_kernel(key_hbm, value_hbm, in_hbm, forget_hbm, tiles_ref, cum_ref, keys, values, gates_in, gates, semaphores):
    copies = fetch((forget_hbm, in_hbm, key_hbm, value_hbm), (gates, gates_in, keys, values), semaphores)
    length = keys.shape[0]
    copies[0].wait()
    gate = gates[...]
    log_forget = jnp.minimum(gate, 0.0) - jnp.log1p(jnp.exp(-jnp.abs(gate)))
    log_forget = jnp.broadcast_to(log_forget, (8, length))
    before = lax.broadcasted_iota(jnp.int32, (length, length), 0)
    after = lax.broadcasted_iota(jnp.int32, (length, length), 1)
    upper = jnp.where(before <= after, 1.0, 0.0).astype(F32)
    cum = jnp.dot(log_forget, upper, precision=lax.Precision.HIGHEST, preferred_element_type=F32)
    cum_ref[...] = cum
    decay = cum[0:1, length - 1 : length]
    copies[1].wait()
    end_weight = decay - cum[0:1] + gates_in[...]
    end_max = jnp.max(end_weight, axis=1, keepdims=True)
    copies[2].wait()
    scaled = (keys[...].astype(F32).T * jnp.exp(end_weight - end_max)).astype(BF16)
    copies[3].wait()
    state = jnp.dot(scaled, values[...], preferred_element_type=F32).astype(BF16)
    places = tiles(*state.shape)
    for place, (row, col) in enumerate(places):
        tiles_ref[place] = state[row : row + TILE[0], col : col + TILE[1]]
    tiles_ref[len(places)] = scalar_tile(end_max, decay)


def pair_kernel(core_ref, both_ref, send_ref):
    core = core_ref[0]
    owners = send_ref.shape[0]
    last = both_ref.shape[1] - 1
    half = last // 2
    per = half // owners
    max_0, decay_0 = scalars_of(both_ref[0, last])
    max_1, decay_1 = scalars_of(both_ref[1, last])
    end_max = jnp.maximum(decay_1 + max_0, max_1)
    scale_0 = jnp.exp(decay_1 + max_0 - end_max)
    scale_1 = jnp.exp(max_1 - end_max)
    scalars = scalar_tile(end_max, decay_0 + decay_1)
    for owner in range(owners):
        for piece in range(per):
            place = core * half + owner * per + piece
            send_ref[owner, piece * 16 : piece * 16 + 16] = (
                scale_0 * both_ref[0, place].astype(F32) + scale_1 * both_ref[1, place].astype(F32)
            ).astype(BF16)
        send_ref[owner, per * 16 : per * 16 + 8] = scalars[0:8]


def prefix_kernel(chip_ref, held_ref, state_ref, max_ref, maxes):
    chips, rows, lanes = state_ref.shape
    state = jnp.zeros((rows, lanes), F32)
    start_max = jnp.full((1, lanes), NEG, F32)
    for chip in range(chips):
        state_ref[chip] = state.astype(BF16)
        maxes[chip] = jnp.broadcast_to(start_max, (8, lanes))
        end_max, decay = scalars_of(held_ref[chip, rows : rows + 8])
        new_max = jnp.maximum(decay + start_max, end_max)
        state = jnp.exp(decay + start_max - new_max) * state + jnp.exp(
            end_max - new_max
        ) * held_ref[chip, 0:rows].astype(F32)
        start_max = new_max
    max_ref[...] = maxes[chip_ref[0]]


def block_kernel(
    query_hbm, key_hbm, value_hbm, in_hbm, gate_hbm, gain_hbm, cum_ref,
    intra_ref, query_ref, gate_ref, stats_ref, keys, values, gates_in, gates, gains, semaphores
):
    copies = fetch(
        (in_hbm, query_hbm, key_hbm, value_hbm, gate_hbm, gain_hbm),
        (gates_in, query_ref, keys, values, gates, gains),
        semaphores,
    )
    length, width = query_ref.shape
    cum_row = cum_ref[0:1]
    cum_col = cum_ref[...].T[:, 0:1]
    at = lax.broadcasted_iota(jnp.int32, (length, length), 0)
    by = lax.broadcasted_iota(jnp.int32, (length, length), 1)
    copies[0].wait()
    log_weight = jnp.where(at >= by, cum_col - cum_row + gates_in[...], NEG)
    local_max = jnp.max(log_weight, axis=1, keepdims=True)
    lane = lax.broadcasted_iota(jnp.int32, stats_ref.shape, 1)
    stats_ref[...] = jnp.where(lane == 0, cum_col, local_max)
    copies[1].wait()
    copies[2].wait()
    scores = lax.dot_general(
        query_ref[...], keys[...], (((1,), (1,)), ((), ())), preferred_element_type=F32
    ) * (1.0 / math.sqrt(width))
    weights = (jnp.exp(log_weight - local_max) * scores).astype(BF16)
    copies[3].wait()
    intra_ref[...] = jnp.dot(weights, values[...], preferred_element_type=F32)
    copies[4].wait()
    copies[5].wait()
    gate_ref[...] = gains[...] * jax.nn.sigmoid(gates[...].astype(F32))


def memory_kernel(
    core_ref, intra_ref, query_ref, gate_ref, stats_ref, tiles_ref, both_ref, max_ref, normed_ref, state
):
    inv_root = 1.0 / math.sqrt(query_ref.shape[1])
    second = core_ref[0] == 1
    chip_max = max_ref[0:1]
    first_max, first_decay = scalars_of(both_ref[0, both_ref.shape[1] - 1])
    moved = jnp.maximum(first_decay + chip_max, first_max)
    start = jnp.where(second, moved, chip_max)
    keep = jnp.where(second, jnp.exp(first_decay + chip_max - moved), 1.0)
    add = jnp.where(second, jnp.exp(first_max - moved), 0.0)
    for place, (row, col) in enumerate(tiles(*state.shape)):
        state[row : row + TILE[0], col : col + TILE[1]] = (
            keep * tiles_ref[place].astype(F32) + add * both_ref[0, place].astype(F32)
        ).astype(BF16)
    local_max = stats_ref[:, 1:2]
    carried_weight = stats_ref[:, 0:1] + start[:, 0:1]
    row_max = jnp.maximum(carried_weight, local_max)
    carried = jnp.dot(query_ref[...], state[...], preferred_element_type=F32)
    memory = (
        jnp.exp(local_max - row_max) * intra_ref[...]
        + (jnp.exp(carried_weight - row_max) * inv_root) * carried
    )
    centred = memory - jnp.mean(memory, axis=1, keepdims=True)
    spread = jnp.mean(centred * centred, axis=1, keepdims=True)
    normed_ref[...] = (centred * lax.rsqrt(spread + 1e-06) * gate_ref[...]).astype(BF16)


def project_kernel(heads, slot_ref, *refs):
    normed, weight_hbm, out_ref, weight, semaphores = refs[:heads], *refs[heads:]
    copies = [
        pltpu.make_async_copy(weight_hbm.at[slot_ref[place]], weight.at[place], semaphores.at[place])
        for place in range(heads)
    ]
    for copy in copies:
        copy.start()
    width = normed[0].shape[1]
    total = jnp.zeros(out_ref.shape, F32)
    for place in range(heads):
        copies[place].wait()
        rows = weight[place].reshape(out_ref.shape[1], width)
        total += lax.dot_general(
            normed[place][...], rows, (((1,), (1,)), ((), ())), preferred_element_type=F32
        )
    out_ref[...] = total.astype(BF16)


def head_gather(block, axis, size):
    def shift(value, by):
        return lax.ppermute(value, axis, [(i, (i + by) % size) for i in range(size)])

    gathered = [(0, block)]
    half = block.shape[0] // 2
    if size == 8:
        far, back = shift(block, 2), shift(block, -2)
        near, behind = shift(block, 1), shift(block, -1)
        gathered += [(-1, near), (1, behind), (-2, far), (2, back)]
        gathered += [(-3, shift(far, 1)), (3, shift(back, -1))]
        first, last, _, _ = lax.optimization_barrier((far[:half], back[half:], near, behind))
        opposite = [shift(first, 2), shift(last, -2)]
    else:
        right = left = block
        if size == 4:
            right, left = shift(block, 1), shift(block, -1)
            gathered += [(-1, right), (1, left)]
        opposite = [shift(right[:half], 1), shift(left[half:], -1)]
    gathered.append((size // 2, jnp.concatenate(opposite, axis=0)))
    return gathered


def local(sizes, queries, key_rows, value_rows, input_gate, forget_gate, norm_gain, output_gate, out_weight):
    planes, columns, cores, heads = sizes
    chips = planes * columns
    length, key_width = queries.shape
    value_width = value_rows.shape[1]
    core = lax.axis_index("c")
    head = lax.axis_index("y")
    chip = lax.axis_index(("z", "x"))
    count = key_width * value_width // (TILE[0] * TILE[1])
    per = count // 2 // chips

    swap = [
        (z * heads + h, ((h + heads // 2) % heads) * heads + z)
        for z in range(planes)
        for h in range(heads)
    ]
    weight = lax.ppermute(out_weight.T, ("z", "y"), swap)
    tile_array = functools.partial(jax.ShapeDtypeStruct, dtype=BF16)
    state_tiles, cum = call(
        front_kernel,
        (tile_array((count + 1, *TILE)), jax.ShapeDtypeStruct((8, length), F32)),
        "hhhh",
        [
            pltpu.VMEM(key_rows.shape, BF16),
            pltpu.VMEM(value_rows.shape, BF16),
            pltpu.VMEM(input_gate.shape, F32),
            pltpu.VMEM(forget_gate.shape, F32),
            pltpu.SemaphoreType.DMA((4,)),
        ],
        vmem=60,
    )(key_rows, value_rows, input_gate, forget_gate)
    both = lax.all_gather(state_tiles, "c")
    send = call(pair_kernel, tile_array((chips, per * TILE[0] + 8, TILE[1])), "sv")(core[None], both)
    weight, send = lax.optimization_barrier((weight, send))
    weight = lax.all_gather(weight, ("z", "x", "c"))
    weight = weight.reshape(planes, columns * cores, *weight.shape[-2:])

    held = lax.all_to_all(send, ("z", "x"), 0, 0, tiled=True)
    intra, query_held, gates, stats = call(
        block_kernel,
        (
            jax.ShapeDtypeStruct(value_rows.shape, F32),
            jax.ShapeDtypeStruct(queries.shape, BF16),
            jax.ShapeDtypeStruct(value_rows.shape, F32),
            jax.ShapeDtypeStruct((length, 128), F32),
        ),
        "hhhhhhv",
        [
            pltpu.VMEM(key_rows.shape, BF16),
            pltpu.VMEM(value_rows.shape, BF16),
            pltpu.VMEM(input_gate.shape, F32),
            pltpu.VMEM(output_gate.shape, BF16),
            pltpu.VMEM((1, value_width), F32),
            pltpu.SemaphoreType.DMA((6,)),
        ],
        flops=2 * length * length * (key_width + value_width),
    )(queries, key_rows, value_rows, input_gate, output_gate, norm_gain[None], cum)
    held, intra = lax.optimization_barrier((held, intra))
    starts, start_max = call(
        prefix_kernel,
        (tile_array((chips, per * TILE[0], TILE[1])), jax.ShapeDtypeStruct((8, TILE[1]), F32)),
        "sv",
        [pltpu.VMEM((chips, 8, TILE[1]), F32)],
    )(chip[None], held)
    back = lax.all_to_all(starts, ("z", "x"), 0, 0, tiled=True)
    start_tiles = lax.all_gather(back, "c").reshape(count, *TILE)
    normed = call(
        memory_kernel,
        tile_array((length, value_width)),
        "svvvvvvv",
        [pltpu.VMEM((key_width, value_width), BF16)],
    )(core[None], intra, query_held, gates, stats, start_tiles, both, start_max)
    gathered = head_gather(normed, "y", heads)
    slots = jnp.stack([(head + place + heads // 2) % heads for place, _ in gathered])
    return call(
        functools.partial(project_kernel, heads),
        tile_array((length, value_width)),
        "s" + "v" * heads + "h",
        [
            pltpu.VMEM((heads, columns * cores, *weight.shape[-2:]), BF16),
            pltpu.SemaphoreType.DMA((heads,)),
        ],
        flops=2 * length * value_width * value_width * heads,
    )(slots.astype(jnp.int32), *[block for _, block in gathered], weight)


def solution(mesh, sizes=(8, 4, 2, 8)):
    grid = Mesh(mesh.devices.reshape(sizes), ("z", "x", "c", "y"))
    seq = ("z", "x", "c")
    in_specs = (
        P(seq, "y"), P(seq, "y"), P(seq, "y"), P("y", seq), P("y", seq), P("y"), P(seq, "y"), P("y", seq)
    )
    return jax.shard_map(
        functools.partial(local, sizes), mesh=grid, in_specs=in_specs, out_specs=P(seq, "y"), check_vma=False
    )
```

```python
import functools
import math

import jax
import jax.numpy as jnp
from jax import lax
from jax.experimental import pallas as pl
from jax.experimental.pallas import tpu as pltpu
from jax.sharding import Mesh, PartitionSpec as P

NEG = -1e30
TILE = (16, 128)
F32 = jnp.float32
BF16 = jnp.bfloat16
VMEM = pl.BlockSpec(memory_space=pltpu.VMEM)
SMEM = pl.BlockSpec(memory_space=pltpu.SMEM)
HBM = pl.BlockSpec(memory_space=pl.ANY)


def call(kernel, out_shape, places, scratch=(), flops=0, moved=2**20, vmem=48):
    return pl.pallas_call(
        kernel,
        out_shape=out_shape,
        in_specs=[{"s": SMEM, "v": VMEM, "h": HBM}[place] for place in places],
        out_specs=jax.tree.map(lambda _: VMEM, out_shape),
        scratch_shapes=list(scratch),
        compiler_params=pltpu.CompilerParams(vmem_limit_bytes=vmem * 2**20),
        cost_estimate=pl.CostEstimate(flops=flops, bytes_accessed=moved, transcendentals=0),
    )


def fetch(refs, held, semaphores):
    copies = [
        pltpu.make_async_copy(ref, buffer, semaphores.at[place])
        for place, (ref, buffer) in enumerate(zip(refs, held))
    ]
    for copy in copies:
        copy.start()
    return copies


def tiles(rows, cols):
    return [(r, c) for r in range(0, rows, TILE[0]) for c in range(0, cols, TILE[1])]


def split3(value):
    high = value.astype(BF16).astype(F32)
    middle = (value - high).astype(BF16).astype(F32)
    return high, middle, value - high - middle


def scalar_tile(end_max, decay):
    rows = lax.broadcasted_iota(jnp.int32, TILE, 0)
    held = jnp.zeros(TILE, F32)
    for place, term in enumerate(split3(end_max) + split3(decay)):
        held = jnp.where(rows == place, jnp.broadcast_to(term, TILE), held)
    return held.astype(BF16)


def scalars_of(tile):
    held = tile.astype(F32)
    end_max = held[0:1] + held[1:2] + held[2:3]
    decay = held[3:4] + held[4:5] + held[5:6]
    return end_max, decay


def front_kernel(key_hbm, value_hbm, in_hbm, forget_hbm, tiles_ref, rows_ref, keys, values, gates_in, gates, semaphores):
    copies = fetch((forget_hbm, in_hbm, key_hbm, value_hbm), (gates, gates_in, keys, values), semaphores)
    length = keys.shape[0]
    copies[0].wait()
    gate = gates[...]
    log_forget = jnp.minimum(gate, 0.0) - jnp.log1p(jnp.exp(-jnp.abs(gate)))
    log_forget = jnp.broadcast_to(log_forget, (8, length))
    before = lax.broadcasted_iota(jnp.int32, (length, length), 0)
    after = lax.broadcasted_iota(jnp.int32, (length, length), 1)
    upper = jnp.where(before <= after, 1.0, 0.0).astype(F32)
    cum = jnp.dot(log_forget, upper, precision=lax.Precision.HIGHEST, preferred_element_type=F32)
    rows_ref[0:8] = cum
    decay = cum[0:1, length - 1 : length]
    copies[1].wait()
    rows_ref[8:16] = jnp.broadcast_to(gates_in[...], (8, length))
    end_weight = decay - cum[0:1] + gates_in[...]
    end_max = jnp.max(end_weight, axis=1, keepdims=True)
    copies[2].wait()
    scaled = (keys[...].astype(F32).T * jnp.exp(end_weight - end_max)).astype(BF16)
    copies[3].wait()
    state = jnp.dot(scaled, values[...], preferred_element_type=F32).astype(BF16)
    places = tiles(*state.shape)
    for place, (row, col) in enumerate(places):
        tiles_ref[place] = state[row : row + TILE[0], col : col + TILE[1]]
    tiles_ref[len(places)] = scalar_tile(end_max, decay)


def pair_kernel(core_ref, both_ref, send_ref):
    core = core_ref[0]
    owners = send_ref.shape[0]
    last = both_ref.shape[1] - 1
    half = last // 2
    per = half // owners
    max_0, decay_0 = scalars_of(both_ref[0, last])
    max_1, decay_1 = scalars_of(both_ref[1, last])
    end_max = jnp.maximum(decay_1 + max_0, max_1)
    scale_0 = jnp.exp(decay_1 + max_0 - end_max)
    scale_1 = jnp.exp(max_1 - end_max)
    scalars = scalar_tile(end_max, decay_0 + decay_1)
    for owner in range(owners):
        for piece in range(per):
            place = core * half + owner * per + piece
            send_ref[owner, piece * 16 : piece * 16 + 16] = (
                scale_0 * both_ref[0, place].astype(F32) + scale_1 * both_ref[1, place].astype(F32)
            ).astype(BF16)
        send_ref[owner, per * 16 : per * 16 + 8] = scalars[0:8]


def prefix_kernel(chip_ref, held_ref, state_ref, max_ref, maxes):
    chips, rows, lanes = state_ref.shape
    state = jnp.zeros((rows, lanes), F32)
    start_max = jnp.full((1, lanes), NEG, F32)
    for chip in range(chips):
        state_ref[chip] = state.astype(BF16)
        maxes[chip] = jnp.broadcast_to(start_max, (8, lanes))
        end_max, decay = scalars_of(held_ref[chip, rows : rows + 8])
        new_max = jnp.maximum(decay + start_max, end_max)
        state = jnp.exp(decay + start_max - new_max) * state + jnp.exp(
            end_max - new_max
        ) * held_ref[chip, 0:rows].astype(F32)
        start_max = new_max
    max_ref[...] = maxes[chip_ref[0]]


def block_kernel(
    query_hbm, key_hbm, value_hbm, rows_ref, intra_ref, query_ref, stats_ref, keys, values, semaphores
):
    copies = fetch((query_hbm, key_hbm, value_hbm), (query_ref, keys, values), semaphores)
    length, width = query_ref.shape
    cum_row = rows_ref[0:1]
    cum_col = rows_ref[0:8].T[:, 0:1]
    at = lax.broadcasted_iota(jnp.int32, (length, length), 0)
    by = lax.broadcasted_iota(jnp.int32, (length, length), 1)
    log_weight = jnp.where(at >= by, cum_col - cum_row + rows_ref[8:9], NEG)
    local_max = jnp.max(log_weight, axis=1, keepdims=True)
    lane = lax.broadcasted_iota(jnp.int32, stats_ref.shape, 1)
    stats_ref[...] = jnp.where(lane == 0, cum_col, local_max)
    copies[0].wait()
    copies[1].wait()
    scores = lax.dot_general(
        query_ref[...], keys[...], (((1,), (1,)), ((), ())), preferred_element_type=F32
    ) * (1.0 / math.sqrt(width))
    weights = (jnp.exp(log_weight - local_max) * scores).astype(BF16)
    copies[2].wait()
    intra_ref[...] = jnp.dot(weights, values[...], preferred_element_type=F32)


def gate_kernel(gain_ref, gate_ref, out_ref):
    out_ref[...] = gain_ref[...] * jax.nn.sigmoid(gate_ref[...].astype(F32))


def memory_kernel(
    core_ref, intra_ref, query_ref, gate_ref, stats_ref, tiles_ref, both_ref, max_ref, normed_ref, state
):
    inv_root = 1.0 / math.sqrt(query_ref.shape[1])
    second = core_ref[0] == 1
    chip_max = max_ref[0:1]
    first_max, first_decay = scalars_of(both_ref[0, both_ref.shape[1] - 1])
    moved = jnp.maximum(first_decay + chip_max, first_max)
    start = jnp.where(second, moved, chip_max)
    keep = jnp.where(second, jnp.exp(first_decay + chip_max - moved), 1.0)
    add = jnp.where(second, jnp.exp(first_max - moved), 0.0)
    for place, (row, col) in enumerate(tiles(*state.shape)):
        state[row : row + TILE[0], col : col + TILE[1]] = (
            keep * tiles_ref[place].astype(F32) + add * both_ref[0, place].astype(F32)
        ).astype(BF16)
    local_max = stats_ref[:, 1:2]
    carried_weight = stats_ref[:, 0:1] + start[:, 0:1]
    row_max = jnp.maximum(carried_weight, local_max)
    carried = jnp.dot(query_ref[...], state[...], preferred_element_type=F32)
    memory = (
        jnp.exp(local_max - row_max) * intra_ref[...]
        + (jnp.exp(carried_weight - row_max) * inv_root) * carried
    )
    centred = memory - jnp.mean(memory, axis=1, keepdims=True)
    spread = jnp.mean(centred * centred, axis=1, keepdims=True)
    normed_ref[...] = (centred * lax.rsqrt(spread + 1e-06) * gate_ref[...]).astype(BF16)


def head_product(normed, weight):
    rows = weight.reshape(-1, weight.shape[-1])
    return lax.dot_general(normed, rows, (((1,), (1,)), ((), ())), preferred_element_type=F32)


def project_kernel(where_ref, weight_hbm, *refs):
    normed, (total_ref, last_ref, weight, semaphores) = refs[:-4], refs[-4:]
    copies = [
        pltpu.make_async_copy(
            weight_hbm.at[where_ref[2 * place], :, where_ref[2 * place + 1]],
            weight.at[place] if place < len(normed) else last_ref,
            semaphores.at[place],
        )
        for place in range(len(normed) + 1)
    ]
    for copy in copies:
        copy.start()
    total = jnp.zeros(total_ref.shape, F32)
    for place, block in enumerate(normed):
        copies[place].wait()
        total += head_product(block[...], weight[place])
    total_ref[...] = total
    copies[-1].wait()


def finish_kernel(total_ref, weight_ref, first_ref, last_ref, out_ref):
    half = first_ref.shape[0]
    for start, part in ((0, first_ref), (half, last_ref)):
        rows = pl.ds(start, half)
        out_ref[rows] = (total_ref[rows] + head_product(part[...], weight_ref[...])).astype(BF16)


def head_gather(block, axis, size):
    def shift(value, by):
        return lax.ppermute(value, axis, [(i, (i + by) % size) for i in range(size)])

    gathered = [(0, block)]
    half = block.shape[0] // 2
    if size == 8:
        far, back = shift(block, 2), shift(block, -2)
        near, behind = shift(block, 1), shift(block, -1)
        gathered += [(-1, near), (1, behind), (-2, far), (2, back)]
        gathered += [(-3, shift(far, 1)), (3, shift(back, -1))]
        first, last, _, _ = lax.optimization_barrier((far[:half], back[half:], near, behind))
        opposite = [shift(first, 2), shift(last, -2)]
    else:
        right = left = block
        if size == 4:
            right, left = shift(block, 1), shift(block, -1)
            gathered += [(-1, right), (1, left)]
        opposite = [shift(right[:half], 1), shift(left[half:], -1)]
    return gathered, opposite


def local(sizes, queries, key_rows, value_rows, input_gate, forget_gate, norm_gain, output_gate, out_weight):
    planes, columns, cores, heads = sizes
    chips = planes * columns
    length, key_width = queries.shape
    value_width = value_rows.shape[1]
    core = lax.axis_index("c")
    head = lax.axis_index("y")
    chip = lax.axis_index(("z", "x"))
    count = key_width * value_width // (TILE[0] * TILE[1])
    per = count // 2 // chips

    offsets = (heads // 2, heads // 2 + 1)
    shards = [
        lax.ppermute(
            out_weight.T,
            ("z", "y"),
            [
                (z * heads + h, (h + offset) % heads * heads + z)
                for z in range(planes)
                for h in range(heads)
            ],
        )
        for offset in offsets
    ]
    tile_array = functools.partial(jax.ShapeDtypeStruct, dtype=BF16)
    state_tiles, rows = call(
        front_kernel,
        (tile_array((count + 1, *TILE)), jax.ShapeDtypeStruct((16, length), F32)),
        "hhhh",
        [
            pltpu.VMEM(key_rows.shape, BF16),
            pltpu.VMEM(value_rows.shape, BF16),
            pltpu.VMEM(input_gate.shape, F32),
            pltpu.VMEM(forget_gate.shape, F32),
            pltpu.SemaphoreType.DMA((4,)),
        ],
        vmem=60,
    )(key_rows, value_rows, input_gate, forget_gate)
    both = lax.all_gather(state_tiles, "c")
    send = call(pair_kernel, tile_array((chips, per * TILE[0] + 8, TILE[1])), "sv")(core[None], both)
    shards, send = lax.optimization_barrier((shards, send))
    groups = [
        [(z * columns + x) * cores + c for z in range(first, planes, 2) for x in range(columns) for c in range(cores)]
        for first in range(2)
    ]
    weight = lax.all_gather(jnp.concatenate(shards, axis=0), ("z", "x", "c"), axis_index_groups=groups)
    weight = weight.reshape(planes // 2, columns * cores, 2, *out_weight.shape[::-1])

    held = lax.all_to_all(send, ("z", "x"), 0, 0, tiled=True)
    intra, query_held, stats = call(
        block_kernel,
        (
            jax.ShapeDtypeStruct(value_rows.shape, F32),
            jax.ShapeDtypeStruct(queries.shape, BF16),
            jax.ShapeDtypeStruct((length, 128), F32),
        ),
        "hhhv",
        [
            pltpu.VMEM(key_rows.shape, BF16),
            pltpu.VMEM(value_rows.shape, BF16),
            pltpu.SemaphoreType.DMA((3,)),
        ],
        flops=2 * length * length * (key_width + value_width),
    )(queries, key_rows, value_rows, rows)
    held, intra = lax.optimization_barrier((held, intra))
    starts, start_max = call(
        prefix_kernel,
        (tile_array((chips, per * TILE[0], TILE[1])), jax.ShapeDtypeStruct((8, TILE[1]), F32)),
        "sv",
        [pltpu.VMEM((chips, 8, TILE[1]), F32)],
    )(chip[None], held)
    back = lax.all_to_all(starts, ("z", "x"), 0, 0, tiled=True)
    gates = call(gate_kernel, jax.ShapeDtypeStruct(value_rows.shape, F32), "vv", moved=2**20)(
        norm_gain[None], output_gate
    )
    back, gates = lax.optimization_barrier((back, gates))
    start_tiles = lax.all_gather(back, "c").reshape(count, *TILE)
    normed = call(
        memory_kernel,
        tile_array((length, value_width)),
        "svvvvvvv",
        [pltpu.VMEM((key_width, value_width), BF16)],
    )(core[None], intra, query_held, gates, stats, start_tiles, both, start_max)
    gathered, opposite = head_gather(normed, "y", heads)
    parity = lax.axis_index("z") % 2
    where = []
    for place in [place for place, _ in gathered] + [heads // 2]:
        owners = [(head + place + offset) % heads for offset in offsets]
        part = (owners[0] % 2 != parity).astype(jnp.int32)
        where += [jnp.where(part == 0, owners[0], owners[1]) // 2, part]
    total, last = call(
        project_kernel,
        (
            jax.ShapeDtypeStruct((length, value_width), F32),
            tile_array((columns * cores, *weight.shape[3:])),
        ),
        "sh" + "v" * len(gathered),
        [
            pltpu.VMEM((len(gathered), columns * cores, *weight.shape[3:]), BF16),
            pltpu.SemaphoreType.DMA((len(gathered) + 1,)),
        ],
        flops=2 * length * value_width * value_width * heads,
        moved=2**23,
    )(jnp.stack(where).astype(jnp.int32), weight, *[block for _, block in gathered])
    return call(finish_kernel, tile_array((length, value_width)), "vvvv")(total, last, *opposite)


def solution(mesh, sizes=(8, 4, 2, 8)):
    grid = Mesh(mesh.devices.reshape(sizes), ("z", "x", "c", "y"))
    seq = ("z", "x", "c")
    in_specs = (
        P(seq, "y"), P(seq, "y"), P(seq, "y"), P("y", seq), P("y", seq), P("y"), P(seq, "y"), P("y", seq)
    )
    return jax.shard_map(
        functools.partial(local, sizes), mesh=grid, in_specs=in_specs, out_specs=P(seq, "y"), check_vma=False
    )
```

```python
import functools
import math

import jax
import jax.numpy as jnp
from jax import lax
from jax.experimental import pallas as pl
from jax.experimental.pallas import tpu as pltpu
from jax.sharding import Mesh, PartitionSpec as P

NEG = -1e30
TILE = (16, 128)
F32 = jnp.float32
BF16 = jnp.bfloat16
VMEM = pl.BlockSpec(memory_space=pltpu.VMEM)
SMEM = pl.BlockSpec(memory_space=pltpu.SMEM)
HBM = pl.BlockSpec(memory_space=pl.ANY)


def call(kernel, out_shape, places, scratch=(), flops=0, moved=2**20, vmem=48):
    return pl.pallas_call(
        kernel,
        out_shape=out_shape,
        in_specs=[{"s": SMEM, "v": VMEM, "h": HBM}[place] for place in places],
        out_specs=jax.tree.map(lambda _: VMEM, out_shape),
        scratch_shapes=list(scratch),
        compiler_params=pltpu.CompilerParams(vmem_limit_bytes=vmem * 2**20),
        cost_estimate=pl.CostEstimate(flops=flops, bytes_accessed=moved, transcendentals=0),
    )


def fetch(refs, held, semaphores):
    copies = [
        pltpu.make_async_copy(ref, buffer, semaphores.at[place])
        for place, (ref, buffer) in enumerate(zip(refs, held))
    ]
    for copy in copies:
        copy.start()
    return copies


def tiles(rows, cols):
    return [(r, c) for r in range(0, rows, TILE[0]) for c in range(0, cols, TILE[1])]


def split3(value):
    high = value.astype(BF16).astype(F32)
    middle = (value - high).astype(BF16).astype(F32)
    return high, middle, value - high - middle


def scalar_tile(end_max, decay):
    rows = lax.broadcasted_iota(jnp.int32, TILE, 0)
    held = jnp.zeros(TILE, F32)
    for place, term in enumerate(split3(end_max) + split3(decay)):
        held = jnp.where(rows == place, jnp.broadcast_to(term, TILE), held)
    return held.astype(BF16)


def scalars_of(tile):
    held = tile.astype(F32)
    end_max = held[0:1] + held[1:2] + held[2:3]
    decay = held[3:4] + held[4:5] + held[5:6]
    return end_max, decay


def front_kernel(key_hbm, value_hbm, in_hbm, forget_hbm, tiles_ref, rows_ref, keys, values, gates_in, gates, semaphores):
    copies = fetch((forget_hbm, in_hbm, key_hbm, value_hbm), (gates, gates_in, keys, values), semaphores)
    length = keys.shape[0]
    copies[0].wait()
    gate = gates[...]
    log_forget = jnp.minimum(gate, 0.0) - jnp.log1p(jnp.exp(-jnp.abs(gate)))
    log_forget = jnp.broadcast_to(log_forget, (8, length))
    before = lax.broadcasted_iota(jnp.int32, (length, length), 0)
    after = lax.broadcasted_iota(jnp.int32, (length, length), 1)
    upper = jnp.where(before <= after, 1.0, 0.0).astype(F32)
    cum = jnp.dot(log_forget, upper, precision=lax.Precision.HIGHEST, preferred_element_type=F32)
    rows_ref[0:8] = cum
    decay = cum[0:1, length - 1 : length]
    copies[1].wait()
    rows_ref[8:16] = jnp.broadcast_to(gates_in[...], (8, length))
    end_weight = decay - cum[0:1] + gates_in[...]
    end_max = jnp.max(end_weight, axis=1, keepdims=True)
    copies[2].wait()
    scaled = (keys[...].astype(F32).T * jnp.exp(end_weight - end_max)).astype(BF16)
    copies[3].wait()
    state = jnp.dot(scaled, values[...], preferred_element_type=F32).astype(BF16)
    places = tiles(*state.shape)
    for place, (row, col) in enumerate(places):
        tiles_ref[place] = state[row : row + TILE[0], col : col + TILE[1]]
    tiles_ref[len(places)] = scalar_tile(end_max, decay)


def pair_kernel(core_ref, both_ref, send_ref):
    core = core_ref[0]
    owners = send_ref.shape[0]
    last = both_ref.shape[1] - 1
    half = last // 2
    per = half // owners
    max_0, decay_0 = scalars_of(both_ref[0, last])
    max_1, decay_1 = scalars_of(both_ref[1, last])
    end_max = jnp.maximum(decay_1 + max_0, max_1)
    scale_0 = jnp.exp(decay_1 + max_0 - end_max)
    scale_1 = jnp.exp(max_1 - end_max)
    scalars = scalar_tile(end_max, decay_0 + decay_1)
    for owner in range(owners):
        for piece in range(per):
            place = core * half + owner * per + piece
            send_ref[owner, piece * 16 : piece * 16 + 16] = (
                scale_0 * both_ref[0, place].astype(F32) + scale_1 * both_ref[1, place].astype(F32)
            ).astype(BF16)
        send_ref[owner, per * 16 : per * 16 + 8] = scalars[0:8]


def prefix_kernel(chip_ref, held_ref, state_ref, max_ref, maxes):
    chips, rows, lanes = state_ref.shape
    state = jnp.zeros((rows, lanes), F32)
    start_max = jnp.full((1, lanes), NEG, F32)
    for chip in range(chips):
        state_ref[chip] = state.astype(BF16)
        maxes[chip] = jnp.broadcast_to(start_max, (8, lanes))
        end_max, decay = scalars_of(held_ref[chip, rows : rows + 8])
        new_max = jnp.maximum(decay + start_max, end_max)
        state = jnp.exp(decay + start_max - new_max) * state + jnp.exp(
            end_max - new_max
        ) * held_ref[chip, 0:rows].astype(F32)
        start_max = new_max
    max_ref[...] = maxes[chip_ref[0]]


def block_kernel(
    query_hbm, key_hbm, value_hbm, rows_ref, intra_ref, query_ref, stats_ref, keys, values, semaphores
):
    copies = fetch((query_hbm, key_hbm, value_hbm), (query_ref, keys, values), semaphores)
    length, width = query_ref.shape
    cum_row = rows_ref[0:1]
    cum_col = rows_ref[0:8].T[:, 0:1]
    at = lax.broadcasted_iota(jnp.int32, (length, length), 0)
    by = lax.broadcasted_iota(jnp.int32, (length, length), 1)
    log_weight = jnp.where(at >= by, cum_col - cum_row + rows_ref[8:9], NEG)
    local_max = jnp.max(log_weight, axis=1, keepdims=True)
    lane = lax.broadcasted_iota(jnp.int32, stats_ref.shape, 1)
    stats_ref[...] = jnp.where(lane == 0, cum_col, local_max)
    copies[0].wait()
    copies[1].wait()
    scores = lax.dot_general(
        query_ref[...], keys[...], (((1,), (1,)), ((), ())), preferred_element_type=F32
    ) * (1.0 / math.sqrt(width))
    weights = (jnp.exp(log_weight - local_max) * scores).astype(BF16)
    copies[2].wait()
    intra_ref[...] = jnp.dot(weights, values[...], preferred_element_type=F32)


def gate_kernel(gain_ref, gate_ref, out_ref):
    out_ref[...] = gain_ref[...] * jax.nn.sigmoid(gate_ref[...].astype(F32))


def memory_kernel(
    core_ref, intra_ref, query_ref, gate_ref, stats_ref, tiles_ref, both_ref, max_ref, normed_ref, state
):
    inv_root = 1.0 / math.sqrt(query_ref.shape[1])
    second = core_ref[0] == 1
    chip_max = max_ref[0:1]
    first_max, first_decay = scalars_of(both_ref[0, both_ref.shape[1] - 1])
    moved = jnp.maximum(first_decay + chip_max, first_max)
    start = jnp.where(second, moved, chip_max)
    keep = jnp.where(second, jnp.exp(first_decay + chip_max - moved), 1.0)
    add = jnp.where(second, jnp.exp(first_max - moved), 0.0)
    for place, (row, col) in enumerate(tiles(*state.shape)):
        state[row : row + TILE[0], col : col + TILE[1]] = (
            keep * tiles_ref[place].astype(F32) + add * both_ref[0, place].astype(F32)
        ).astype(BF16)
    local_max = stats_ref[:, 1:2]
    carried_weight = stats_ref[:, 0:1] + start[:, 0:1]
    row_max = jnp.maximum(carried_weight, local_max)
    carried = jnp.dot(query_ref[...], state[...], preferred_element_type=F32)
    memory = (
        jnp.exp(local_max - row_max) * intra_ref[...]
        + (jnp.exp(carried_weight - row_max) * inv_root) * carried
    )
    centred = memory - jnp.mean(memory, axis=1, keepdims=True)
    spread = jnp.mean(centred * centred, axis=1, keepdims=True)
    normed_ref[...] = (centred * lax.rsqrt(spread + 1e-06) * gate_ref[...]).astype(BF16)


def head_product(normed, weight):
    rows = weight.reshape(-1, weight.shape[-1])
    return lax.dot_general(normed, rows, (((1,), (1,)), ((), ())), preferred_element_type=F32)


def project_kernel(where_ref, weight_hbm, *refs):
    normed, (total_ref, last_ref, weight, semaphores) = refs[:-4], refs[-4:]
    copies = [
        pltpu.make_async_copy(
            weight_hbm.at[where_ref[2 * place], :, where_ref[2 * place + 1]],
            weight.at[place] if place < len(normed) else last_ref,
            semaphores.at[place],
        )
        for place in range(len(normed) + 1)
    ]
    for copy in copies:
        copy.start()
    total = jnp.zeros(total_ref.shape, F32)
    for place, block in enumerate(normed):
        copies[place].wait()
        total += head_product(block[...], weight[place])
    total_ref[...] = total
    copies[-1].wait()


def finish_kernel(total_ref, weight_ref, first_ref, last_ref, out_ref):
    half = first_ref.shape[0]
    for start, part in ((0, first_ref), (half, last_ref)):
        rows = pl.ds(start, half)
        out_ref[rows] = (total_ref[rows] + head_product(part[...], weight_ref[...])).astype(BF16)


def head_gather(block, axis, size):
    def shift(value, by):
        return lax.ppermute(value, axis, [(i, (i + by) % size) for i in range(size)])

    gathered = [(0, block)]
    half = block.shape[0] // 2
    if size == 8:
        far, back = shift(block, 2), shift(block, -2)
        near, behind = shift(block, 1), shift(block, -1)
        gathered += [(-1, near), (1, behind), (-2, far), (2, back)]
        gathered += [(-3, shift(far, 1)), (3, shift(back, -1))]
        opposite = [shift(far[:half], 2), shift(back[half:], -2)]
    else:
        right = left = block
        if size == 4:
            right, left = shift(block, 1), shift(block, -1)
            gathered += [(-1, right), (1, left)]
        opposite = [shift(right[:half], 1), shift(left[half:], -1)]
    return gathered, opposite


def local(sizes, queries, key_rows, value_rows, input_gate, forget_gate, norm_gain, output_gate, out_weight):
    planes, columns, cores, heads = sizes
    chips = planes * columns
    length, key_width = queries.shape
    value_width = value_rows.shape[1]
    core = lax.axis_index("c")
    head = lax.axis_index("y")
    chip = lax.axis_index(("z", "x"))
    count = key_width * value_width // (TILE[0] * TILE[1])
    per = count // 2 // chips

    offsets = (heads // 2 + 1, heads // 2)
    shards = [
        lax.ppermute(
            out_weight.T,
            ("z", "y"),
            [
                (z * heads + h, (h + offset) % heads * heads + z)
                for z in range(planes)
                for h in range(heads)
            ],
        )
        for offset in offsets
    ]
    tile_array = functools.partial(jax.ShapeDtypeStruct, dtype=BF16)
    state_tiles, rows = call(
        front_kernel,
        (tile_array((count + 1, *TILE)), jax.ShapeDtypeStruct((16, length), F32)),
        "hhhh",
        [
            pltpu.VMEM(key_rows.shape, BF16),
            pltpu.VMEM(value_rows.shape, BF16),
            pltpu.VMEM(input_gate.shape, F32),
            pltpu.VMEM(forget_gate.shape, F32),
            pltpu.SemaphoreType.DMA((4,)),
        ],
        vmem=60,
    )(key_rows, value_rows, input_gate, forget_gate)
    both = lax.all_gather(state_tiles, "c")
    send = call(pair_kernel, tile_array((chips, per * TILE[0] + 8, TILE[1])), "sv")(core[None], both)
    shards, send = lax.optimization_barrier((shards, send))
    groups = [
        [(z * columns + x) * cores + c for z in range(first, planes, 2) for x in range(columns) for c in range(cores)]
        for first in range(2)
    ]
    weight = lax.all_gather(jnp.concatenate(shards, axis=0), ("z", "x", "c"), axis_index_groups=groups)
    weight = weight.reshape(planes // 2, columns * cores, 2, *out_weight.shape[::-1])

    held = lax.all_to_all(send, ("z", "x"), 0, 0, tiled=True)
    intra, query_held, stats = call(
        block_kernel,
        (
            jax.ShapeDtypeStruct(value_rows.shape, F32),
            jax.ShapeDtypeStruct(queries.shape, BF16),
            jax.ShapeDtypeStruct((length, 128), F32),
        ),
        "hhhv",
        [
            pltpu.VMEM(key_rows.shape, BF16),
            pltpu.VMEM(value_rows.shape, BF16),
            pltpu.SemaphoreType.DMA((3,)),
        ],
        flops=2 * length * length * (key_width + value_width),
    )(queries, key_rows, value_rows, rows)
    held, intra = lax.optimization_barrier((held, intra))
    starts, start_max = call(
        prefix_kernel,
        (tile_array((chips, per * TILE[0], TILE[1])), jax.ShapeDtypeStruct((8, TILE[1]), F32)),
        "sv",
        [pltpu.VMEM((chips, 8, TILE[1]), F32)],
    )(chip[None], held)
    back = lax.all_to_all(starts, ("z", "x"), 0, 0, tiled=True)
    gates = call(gate_kernel, jax.ShapeDtypeStruct(value_rows.shape, F32), "vv", moved=2**20)(
        norm_gain[None], output_gate
    )
    back, gates = lax.optimization_barrier((back, gates))
    start_tiles = lax.all_gather(back, "c").reshape(count, *TILE)
    normed = call(
        memory_kernel,
        tile_array((length, value_width)),
        "svvvvvvv",
        [pltpu.VMEM((key_width, value_width), BF16)],
    )(core[None], intra, query_held, gates, stats, start_tiles, both, start_max)
    gathered, opposite = head_gather(normed, "y", heads)
    parity = lax.axis_index("z") % 2
    where = []
    for place in [place for place, _ in gathered] + [heads // 2]:
        owners = [(head + place + offset) % heads for offset in offsets]
        part = (owners[0] % 2 != parity).astype(jnp.int32)
        where += [jnp.where(part == 0, owners[0], owners[1]) // 2, part]
    total, last = call(
        project_kernel,
        (
            jax.ShapeDtypeStruct((length, value_width), F32),
            tile_array((columns * cores, *weight.shape[3:])),
        ),
        "sh" + "v" * len(gathered),
        [
            pltpu.VMEM((len(gathered), columns * cores, *weight.shape[3:]), BF16),
            pltpu.SemaphoreType.DMA((len(gathered) + 1,)),
        ],
        flops=2 * length * value_width * value_width * heads,
        moved=2**23,
    )(jnp.stack(where).astype(jnp.int32), weight, *[block for _, block in gathered])
    return call(finish_kernel, tile_array((length, value_width)), "vvvv")(total, last, *opposite)


def solution(mesh, sizes=(8, 4, 2, 8)):
    grid = Mesh(mesh.devices.reshape(sizes), ("z", "x", "c", "y"))
    seq = ("z", "x", "c")
    in_specs = (
        P(seq, "y"), P(seq, "y"), P(seq, "y"), P("y", seq), P("y", seq), P("y"), P(seq, "y"), P("y", seq)
    )
    return jax.shard_map(
        functools.partial(local, sizes), mesh=grid, in_specs=in_specs, out_specs=P(seq, "y"), check_vma=False
    )
```

```python
import functools
import math

import jax
import jax.numpy as jnp
from jax import lax
from jax.experimental import pallas as pl
from jax.experimental.pallas import tpu as pltpu
from jax.sharding import Mesh, PartitionSpec as P

NEG = -1e30
TILE = (16, 128)
F32 = jnp.float32
BF16 = jnp.bfloat16
VMEM = pl.BlockSpec(memory_space=pltpu.VMEM)
SMEM = pl.BlockSpec(memory_space=pltpu.SMEM)
HBM = pl.BlockSpec(memory_space=pl.ANY)


def call(kernel, out_shape, places, scratch=(), flops=0, moved=2**20, vmem=48):
    return pl.pallas_call(
        kernel,
        out_shape=out_shape,
        in_specs=[{"s": SMEM, "v": VMEM, "h": HBM}[place] for place in places],
        out_specs=jax.tree.map(lambda _: VMEM, out_shape),
        scratch_shapes=list(scratch),
        compiler_params=pltpu.CompilerParams(vmem_limit_bytes=vmem * 2**20),
        cost_estimate=pl.CostEstimate(flops=flops, bytes_accessed=moved, transcendentals=0),
    )


def fetch(refs, held, semaphores):
    copies = [
        pltpu.make_async_copy(ref, buffer, semaphores.at[place])
        for place, (ref, buffer) in enumerate(zip(refs, held))
    ]
    for copy in copies:
        copy.start()
    return copies


def tiles(rows, cols):
    return [(r, c) for r in range(0, rows, TILE[0]) for c in range(0, cols, TILE[1])]


def split3(value):
    high = value.astype(BF16).astype(F32)
    middle = (value - high).astype(BF16).astype(F32)
    return high, middle, value - high - middle


def scalar_tile(end_max, decay):
    rows = lax.broadcasted_iota(jnp.int32, TILE, 0)
    held = jnp.zeros(TILE, F32)
    for place, term in enumerate(split3(end_max) + split3(decay)):
        held = jnp.where(rows == place, jnp.broadcast_to(term, TILE), held)
    return held.astype(BF16)


def scalars_of(tile):
    held = tile.astype(F32)
    end_max = held[0:1] + held[1:2] + held[2:3]
    decay = held[3:4] + held[4:5] + held[5:6]
    return end_max, decay


def front_kernel(key_hbm, value_hbm, in_hbm, forget_hbm, tiles_ref, rows_ref, keys, values, gates_in, gates, semaphores):
    copies = fetch((forget_hbm, in_hbm, key_hbm, value_hbm), (gates, gates_in, keys, values), semaphores)
    length = keys.shape[0]
    copies[0].wait()
    gate = gates[...]
    log_forget = jnp.minimum(gate, 0.0) - jnp.log1p(jnp.exp(-jnp.abs(gate)))
    log_forget = jnp.broadcast_to(log_forget, (8, length))
    before = lax.broadcasted_iota(jnp.int32, (length, length), 0)
    after = lax.broadcasted_iota(jnp.int32, (length, length), 1)
    upper = jnp.where(before <= after, 1.0, 0.0).astype(F32)
    cum = jnp.dot(log_forget, upper, precision=lax.Precision.HIGHEST, preferred_element_type=F32)
    rows_ref[0:8] = cum
    decay = cum[0:1, length - 1 : length]
    copies[1].wait()
    rows_ref[8:16] = jnp.broadcast_to(gates_in[...], (8, length))
    end_weight = decay - cum[0:1] + gates_in[...]
    end_max = jnp.max(end_weight, axis=1, keepdims=True)
    copies[2].wait()
    scaled = (keys[...].astype(F32).T * jnp.exp(end_weight - end_max)).astype(BF16)
    copies[3].wait()
    state = jnp.dot(scaled, values[...], preferred_element_type=F32).astype(BF16)
    places = tiles(*state.shape)
    for place, (row, col) in enumerate(places):
        tiles_ref[place] = state[row : row + TILE[0], col : col + TILE[1]]
    tiles_ref[len(places)] = scalar_tile(end_max, decay)


def pair_kernel(core_ref, both_ref, send_ref):
    core = core_ref[0]
    owners = send_ref.shape[0]
    last = both_ref.shape[1] - 1
    half = last // 2
    per = half // owners
    max_0, decay_0 = scalars_of(both_ref[0, last])
    max_1, decay_1 = scalars_of(both_ref[1, last])
    end_max = jnp.maximum(decay_1 + max_0, max_1)
    scale_0 = jnp.exp(decay_1 + max_0 - end_max)
    scale_1 = jnp.exp(max_1 - end_max)
    scalars = scalar_tile(end_max, decay_0 + decay_1)
    for owner in range(owners):
        for piece in range(per):
            place = core * half + owner * per + piece
            send_ref[owner, piece * 16 : piece * 16 + 16] = (
                scale_0 * both_ref[0, place].astype(F32) + scale_1 * both_ref[1, place].astype(F32)
            ).astype(BF16)
        send_ref[owner, per * 16 : per * 16 + 8] = scalars[0:8]


def prefix_kernel(chip_ref, held_ref, state_ref, max_ref, maxes):
    chips, rows, lanes = state_ref.shape
    state = jnp.zeros((rows, lanes), F32)
    start_max = jnp.full((1, lanes), NEG, F32)
    for chip in range(chips):
        state_ref[chip] = state.astype(BF16)
        maxes[chip] = jnp.broadcast_to(start_max, (8, lanes))
        end_max, decay = scalars_of(held_ref[chip, rows : rows + 8])
        new_max = jnp.maximum(decay + start_max, end_max)
        state = jnp.exp(decay + start_max - new_max) * state + jnp.exp(
            end_max - new_max
        ) * held_ref[chip, 0:rows].astype(F32)
        start_max = new_max
    max_ref[...] = maxes[chip_ref[0]]


def block_kernel(
    query_hbm, key_hbm, value_hbm, rows_ref, intra_ref, query_ref, stats_ref, keys, values, semaphores
):
    copies = fetch((query_hbm, key_hbm, value_hbm), (query_ref, keys, values), semaphores)
    length, width = query_ref.shape
    cum_row = rows_ref[0:1]
    cum_col = rows_ref[0:8].T[:, 0:1]
    at = lax.broadcasted_iota(jnp.int32, (length, length), 0)
    by = lax.broadcasted_iota(jnp.int32, (length, length), 1)
    log_weight = jnp.where(at >= by, cum_col - cum_row + rows_ref[8:9], NEG)
    local_max = jnp.max(log_weight, axis=1, keepdims=True)
    lane = lax.broadcasted_iota(jnp.int32, stats_ref.shape, 1)
    stats_ref[...] = jnp.where(lane == 0, cum_col, local_max)
    copies[0].wait()
    copies[1].wait()
    scores = lax.dot_general(
        query_ref[...], keys[...], (((1,), (1,)), ((), ())), preferred_element_type=F32
    ) * (1.0 / math.sqrt(width))
    weights = (jnp.exp(log_weight - local_max) * scores).astype(BF16)
    copies[2].wait()
    intra_ref[...] = jnp.dot(weights, values[...], preferred_element_type=F32)


def gate_kernel(gain_ref, gate_ref, out_ref):
    out_ref[...] = gain_ref[...] * jax.nn.sigmoid(gate_ref[...].astype(F32))


def memory_kernel(
    core_ref, intra_ref, query_ref, gate_ref, stats_ref, tiles_ref, both_ref, max_ref, normed_ref, state
):
    inv_root = 1.0 / math.sqrt(query_ref.shape[1])
    second = core_ref[0] == 1
    chip_max = max_ref[0:1]
    first_max, first_decay = scalars_of(both_ref[0, both_ref.shape[1] - 1])
    moved = jnp.maximum(first_decay + chip_max, first_max)
    start = jnp.where(second, moved, chip_max)
    keep = jnp.where(second, jnp.exp(first_decay + chip_max - moved), 1.0)
    add = jnp.where(second, jnp.exp(first_max - moved), 0.0)
    for place, (row, col) in enumerate(tiles(*state.shape)):
        state[row : row + TILE[0], col : col + TILE[1]] = (
            keep * tiles_ref[place].astype(F32) + add * both_ref[0, place].astype(F32)
        ).astype(BF16)
    local_max = stats_ref[:, 1:2]
    carried_weight = stats_ref[:, 0:1] + start[:, 0:1]
    row_max = jnp.maximum(carried_weight, local_max)
    carried = jnp.dot(query_ref[...], state[...], preferred_element_type=F32)
    memory = (
        jnp.exp(local_max - row_max) * intra_ref[...]
        + (jnp.exp(carried_weight - row_max) * inv_root) * carried
    )
    centred = memory - jnp.mean(memory, axis=1, keepdims=True)
    spread = jnp.mean(centred * centred, axis=1, keepdims=True)
    normed_ref[...] = (centred * lax.rsqrt(spread + 1e-06) * gate_ref[...]).astype(BF16)


def head_product(normed, weight):
    rows = weight.reshape(-1, weight.shape[-1])
    return lax.dot_general(normed, rows, (((1,), (1,)), ((), ())), preferred_element_type=F32)


def project_kernel(where_ref, weight_hbm, *refs):
    normed, (total_ref, last_ref, weight, semaphores) = refs[:-4], refs[-4:]
    copies = [
        pltpu.make_async_copy(
            weight_hbm.at[where_ref[2 * place], :, where_ref[2 * place + 1]],
            weight.at[place] if place < len(normed) else last_ref,
            semaphores.at[place],
        )
        for place in range(len(normed) + 1)
    ]
    for copy in copies:
        copy.start()
    total = jnp.zeros(total_ref.shape, F32)
    for place, block in enumerate(normed):
        copies[place].wait()
        total += head_product(block[...], weight[place])
    total_ref[...] = total
    copies[-1].wait()


def finish_kernel(total_ref, weight_ref, first_ref, last_ref, out_ref):
    half = first_ref.shape[0]
    for start, part in ((0, first_ref), (half, last_ref)):
        rows = pl.ds(start, half)
        out_ref[rows] = (total_ref[rows] + head_product(part[...], weight_ref[...])).astype(BF16)


def head_gather(block, axis, size):
    def shift(value, by):
        moves = [(c * size + i, c * size + (i + by * (1 - 2 * c)) % size) for c in range(2) for i in range(size)]
        return lax.ppermute(value, ("c", axis), moves)

    gathered = [(0, block)]
    half = block.shape[0] // 2
    if size == 8:
        far, back = shift(block, 2), shift(block, -2)
        near, behind = shift(block, 1), shift(block, -1)
        gathered += [(-1, near), (1, behind), (-2, far), (2, back)]
        gathered += [(-3, shift(far, 1)), (3, shift(back, -1))]
        opposite = [shift(far[:half], 2), shift(back[half:], -2)]
    else:
        right = left = block
        if size == 4:
            right, left = shift(block, 1), shift(block, -1)
            gathered += [(-1, right), (1, left)]
        opposite = [shift(right[:half], 1), shift(left[half:], -1)]
    return gathered, opposite


def local(sizes, queries, key_rows, value_rows, input_gate, forget_gate, norm_gain, output_gate, out_weight):
    planes, columns, cores, heads = sizes
    chips = planes * columns
    length, key_width = queries.shape
    value_width = value_rows.shape[1]
    core = lax.axis_index("c")
    head = lax.axis_index("y")
    chip = lax.axis_index(("z", "x"))
    count = key_width * value_width // (TILE[0] * TILE[1])
    per = count // 2 // chips

    offsets = (heads // 2 + 1, heads // 2)
    shards = [
        lax.ppermute(
            out_weight.T,
            ("z", "y"),
            [
                (z * heads + h, (h + offset) % heads * heads + z)
                for z in range(planes)
                for h in range(heads)
            ],
        )
        for offset in offsets
    ]
    tile_array = functools.partial(jax.ShapeDtypeStruct, dtype=BF16)
    state_tiles, rows = call(
        front_kernel,
        (tile_array((count + 1, *TILE)), jax.ShapeDtypeStruct((16, length), F32)),
        "hhhh",
        [
            pltpu.VMEM(key_rows.shape, BF16),
            pltpu.VMEM(value_rows.shape, BF16),
            pltpu.VMEM(input_gate.shape, F32),
            pltpu.VMEM(forget_gate.shape, F32),
            pltpu.SemaphoreType.DMA((4,)),
        ],
        vmem=60,
    )(key_rows, value_rows, input_gate, forget_gate)
    both = lax.all_gather(state_tiles, "c")
    send = call(pair_kernel, tile_array((chips, per * TILE[0] + 8, TILE[1])), "sv")(core[None], both)
    shards, send = lax.optimization_barrier((shards, send))
    groups = [
        [(z * columns + x) * cores + c for z in range(first, planes, 2) for x in range(columns) for c in range(cores)]
        for first in range(2)
    ]
    weight = lax.all_gather(jnp.concatenate(shards, axis=0), ("z", "x", "c"), axis_index_groups=groups)
    weight = weight.reshape(planes // 2, columns * cores, 2, *out_weight.shape[::-1])

    held = lax.all_to_all(send, ("z", "x"), 0, 0, tiled=True)
    intra, query_held, stats = call(
        block_kernel,
        (
            jax.ShapeDtypeStruct(value_rows.shape, F32),
            jax.ShapeDtypeStruct(queries.shape, BF16),
            jax.ShapeDtypeStruct((length, 128), F32),
        ),
        "hhhv",
        [
            pltpu.VMEM(key_rows.shape, BF16),
            pltpu.VMEM(value_rows.shape, BF16),
            pltpu.SemaphoreType.DMA((3,)),
        ],
        flops=2 * length * length * (key_width + value_width),
    )(queries, key_rows, value_rows, rows)
    held, intra = lax.optimization_barrier((held, intra))
    starts, start_max = call(
        prefix_kernel,
        (tile_array((chips, per * TILE[0], TILE[1])), jax.ShapeDtypeStruct((8, TILE[1]), F32)),
        "sv",
        [pltpu.VMEM((chips, 8, TILE[1]), F32)],
    )(chip[None], held)
    back = lax.all_to_all(starts, ("z", "x"), 0, 0, tiled=True)
    gates = call(gate_kernel, jax.ShapeDtypeStruct(value_rows.shape, F32), "vv", moved=2**20)(
        norm_gain[None], output_gate
    )
    back, gates = lax.optimization_barrier((back, gates))
    start_tiles = lax.all_gather(back, "c").reshape(count, *TILE)
    normed = call(
        memory_kernel,
        tile_array((length, value_width)),
        "svvvvvvv",
        [pltpu.VMEM((key_width, value_width), BF16)],
    )(core[None], intra, query_held, gates, stats, start_tiles, both, start_max)
    gathered, opposite = head_gather(normed, "y", heads)
    parity = lax.axis_index("z") % 2
    way = 1 - 2 * core
    where = []
    for place in [place for place, _ in gathered] + [heads // 2]:
        owners = [(head + way * place + offset) % heads for offset in offsets]
        part = (owners[0] % 2 != parity).astype(jnp.int32)
        where += [jnp.where(part == 0, owners[0], owners[1]) // 2, part]
    total, last = call(
        project_kernel,
        (
            jax.ShapeDtypeStruct((length, value_width), F32),
            tile_array((columns * cores, *weight.shape[3:])),
        ),
        "sh" + "v" * len(gathered),
        [
            pltpu.VMEM((len(gathered), columns * cores, *weight.shape[3:]), BF16),
            pltpu.SemaphoreType.DMA((len(gathered) + 1,)),
        ],
        flops=2 * length * value_width * value_width * heads,
        moved=2**23,
    )(jnp.stack(where).astype(jnp.int32), weight, *[block for _, block in gathered])
    return call(finish_kernel, tile_array((length, value_width)), "vvvv")(total, last, *opposite)


def solution(mesh, sizes=(8, 4, 2, 8)):
    grid = Mesh(mesh.devices.reshape(sizes), ("z", "x", "c", "y"))
    seq = ("z", "x", "c")
    in_specs = (
        P(seq, "y"), P(seq, "y"), P(seq, "y"), P("y", seq), P("y", seq), P("y"), P(seq, "y"), P("y", seq)
    )
    return jax.shard_map(
        functools.partial(local, sizes), mesh=grid, in_specs=in_specs, out_specs=P(seq, "y"), check_vma=False
    )
```

```python
import functools
import math

import jax
import jax.numpy as jnp
from jax import lax
from jax.experimental import pallas as pl
from jax.experimental.pallas import tpu as pltpu
from jax.sharding import Mesh, PartitionSpec as P

NEG = -1e30
TILE = (16, 128)
F32 = jnp.float32
BF16 = jnp.bfloat16
VMEM = pl.BlockSpec(memory_space=pltpu.VMEM)
SMEM = pl.BlockSpec(memory_space=pltpu.SMEM)
HBM = pl.BlockSpec(memory_space=pl.ANY)


def call(kernel, out_shape, places, scratch=(), flops=0, moved=2**20, vmem=48):
    return pl.pallas_call(
        kernel,
        out_shape=out_shape,
        in_specs=[{"s": SMEM, "v": VMEM, "h": HBM}[place] for place in places],
        out_specs=jax.tree.map(lambda _: VMEM, out_shape),
        scratch_shapes=list(scratch),
        compiler_params=pltpu.CompilerParams(vmem_limit_bytes=vmem * 2**20),
        cost_estimate=pl.CostEstimate(flops=flops, bytes_accessed=moved, transcendentals=0),
    )


def fetch(refs, held, semaphores):
    copies = [
        pltpu.make_async_copy(ref, buffer, semaphores.at[place])
        for place, (ref, buffer) in enumerate(zip(refs, held))
    ]
    for copy in copies:
        copy.start()
    return copies


def tiles(rows, cols):
    return [(r, c) for r in range(0, rows, TILE[0]) for c in range(0, cols, TILE[1])]


def split3(value):
    high = value.astype(BF16).astype(F32)
    middle = (value - high).astype(BF16).astype(F32)
    return high, middle, value - high - middle


def scalar_tile(end_max, decay):
    rows = lax.broadcasted_iota(jnp.int32, TILE, 0)
    held = jnp.zeros(TILE, F32)
    for place, term in enumerate(split3(end_max) + split3(decay)):
        held = jnp.where(rows == place, jnp.broadcast_to(term, TILE), held)
    return held.astype(BF16)


def scalars_of(tile):
    held = tile.astype(F32)
    end_max = held[0:1] + held[1:2] + held[2:3]
    decay = held[3:4] + held[4:5] + held[5:6]
    return end_max, decay


def front_kernel(key_hbm, value_hbm, in_hbm, forget_hbm, tiles_ref, rows_ref, keys, values, gates_in, gates, semaphores):
    copies = fetch((forget_hbm, in_hbm, key_hbm, value_hbm), (gates, gates_in, keys, values), semaphores)
    length = keys.shape[0]
    copies[0].wait()
    gate = gates[...]
    log_forget = jnp.minimum(gate, 0.0) - jnp.log1p(jnp.exp(-jnp.abs(gate)))
    log_forget = jnp.broadcast_to(log_forget, (8, length))
    before = lax.broadcasted_iota(jnp.int32, (length, length), 0)
    after = lax.broadcasted_iota(jnp.int32, (length, length), 1)
    upper = jnp.where(before <= after, 1.0, 0.0).astype(F32)
    cum = jnp.dot(log_forget, upper, precision=lax.Precision.HIGHEST, preferred_element_type=F32)
    rows_ref[0:8] = cum
    decay = cum[0:1, length - 1 : length]
    copies[1].wait()
    rows_ref[8:16] = jnp.broadcast_to(gates_in[...], (8, length))
    end_weight = decay - cum[0:1] + gates_in[...]
    end_max = jnp.max(end_weight, axis=1, keepdims=True)
    copies[2].wait()
    scaled = (keys[...].astype(F32).T * jnp.exp(end_weight - end_max)).astype(BF16)
    copies[3].wait()
    state = jnp.dot(scaled, values[...], preferred_element_type=F32).astype(BF16)
    places = tiles(*state.shape)
    for place, (row, col) in enumerate(places):
        tiles_ref[place] = state[row : row + TILE[0], col : col + TILE[1]]
    tiles_ref[len(places)] = scalar_tile(end_max, decay)


def pair_kernel(core_ref, both_ref, send_ref):
    core = core_ref[0]
    owners = send_ref.shape[0]
    last = both_ref.shape[1] - 1
    half = last // 2
    per = half // owners
    max_0, decay_0 = scalars_of(both_ref[0, last])
    max_1, decay_1 = scalars_of(both_ref[1, last])
    end_max = jnp.maximum(decay_1 + max_0, max_1)
    scale_0 = jnp.exp(decay_1 + max_0 - end_max)
    scale_1 = jnp.exp(max_1 - end_max)
    scalars = scalar_tile(end_max, decay_0 + decay_1)
    for owner in range(owners):
        for piece in range(per):
            place = core * half + owner * per + piece
            send_ref[owner, piece * 16 : piece * 16 + 16] = (
                scale_0 * both_ref[0, place].astype(F32) + scale_1 * both_ref[1, place].astype(F32)
            ).astype(BF16)
        send_ref[owner, per * 16 : per * 16 + 8] = scalars[0:8]


def prefix_kernel(chip_ref, held_ref, state_ref, max_ref, maxes):
    chips, rows, lanes = state_ref.shape
    state = jnp.zeros((rows, lanes), F32)
    start_max = jnp.full((1, lanes), NEG, F32)
    for chip in range(chips):
        state_ref[chip] = state.astype(BF16)
        maxes[chip] = jnp.broadcast_to(start_max, (8, lanes))
        end_max, decay = scalars_of(held_ref[chip, rows : rows + 8])
        new_max = jnp.maximum(decay + start_max, end_max)
        state = jnp.exp(decay + start_max - new_max) * state + jnp.exp(
            end_max - new_max
        ) * held_ref[chip, 0:rows].astype(F32)
        start_max = new_max
    max_ref[...] = maxes[chip_ref[0]]


def block_kernel(
    query_hbm, key_hbm, value_hbm, rows_ref, intra_ref, query_ref, stats_ref, keys, values, semaphores
):
    copies = fetch((query_hbm, key_hbm, value_hbm), (query_ref, keys, values), semaphores)
    length, width = query_ref.shape
    cum_row = rows_ref[0:1]
    cum_col = rows_ref[0:8].T[:, 0:1]
    at = lax.broadcasted_iota(jnp.int32, (length, length), 0)
    by = lax.broadcasted_iota(jnp.int32, (length, length), 1)
    log_weight = jnp.where(at >= by, cum_col - cum_row + rows_ref[8:9], NEG)
    local_max = jnp.max(log_weight, axis=1, keepdims=True)
    lane = lax.broadcasted_iota(jnp.int32, stats_ref.shape, 1)
    stats_ref[...] = jnp.where(lane == 0, cum_col, local_max)
    copies[0].wait()
    copies[1].wait()
    scores = lax.dot_general(
        query_ref[...], keys[...], (((1,), (1,)), ((), ())), preferred_element_type=F32
    ) * (1.0 / math.sqrt(width))
    weights = (jnp.exp(log_weight - local_max) * scores).astype(BF16)
    copies[2].wait()
    intra_ref[...] = jnp.dot(weights, values[...], preferred_element_type=F32)


def gate_kernel(gain_ref, gate_ref, out_ref):
    out_ref[...] = gain_ref[...] * jax.nn.sigmoid(gate_ref[...].astype(F32))


def memory_kernel(
    core_ref, intra_ref, query_ref, gate_ref, stats_ref, tiles_ref, both_ref, max_ref, normed_ref, state
):
    inv_root = 1.0 / math.sqrt(query_ref.shape[1])
    second = core_ref[0] == 1
    chip_max = max_ref[0:1]
    first_max, first_decay = scalars_of(both_ref[0, both_ref.shape[1] - 1])
    moved = jnp.maximum(first_decay + chip_max, first_max)
    start = jnp.where(second, moved, chip_max)
    keep = jnp.where(second, jnp.exp(first_decay + chip_max - moved), 1.0)
    add = jnp.where(second, jnp.exp(first_max - moved), 0.0)
    for place, (row, col) in enumerate(tiles(*state.shape)):
        state[row : row + TILE[0], col : col + TILE[1]] = (
            keep * tiles_ref[place].astype(F32) + add * both_ref[0, place].astype(F32)
        ).astype(BF16)
    local_max = stats_ref[:, 1:2]
    carried_weight = stats_ref[:, 0:1] + start[:, 0:1]
    row_max = jnp.maximum(carried_weight, local_max)
    carried = jnp.dot(query_ref[...], state[...], preferred_element_type=F32)
    memory = (
        jnp.exp(local_max - row_max) * intra_ref[...]
        + (jnp.exp(carried_weight - row_max) * inv_root) * carried
    )
    centred = memory - jnp.mean(memory, axis=1, keepdims=True)
    spread = jnp.mean(centred * centred, axis=1, keepdims=True)
    normed_ref[...] = (centred * lax.rsqrt(spread + 1e-06) * gate_ref[...]).astype(BF16)


def head_product(normed, weight):
    rows = weight.reshape(-1, weight.shape[-1])
    return lax.dot_general(normed, rows, (((1,), (1,)), ((), ())), preferred_element_type=F32)


def project_kernel(where_ref, weight_hbm, *refs):
    normed, (total_ref, last_ref, weight, semaphores) = refs[:-4], refs[-4:]
    copies = [
        pltpu.make_async_copy(
            weight_hbm.at[where_ref[2 * place], :, where_ref[2 * place + 1]],
            weight.at[place] if place < len(normed) else last_ref,
            semaphores.at[place],
        )
        for place in range(len(normed) + 1)
    ]
    for copy in copies:
        copy.start()
    total = jnp.zeros(total_ref.shape, F32)
    for place, block in enumerate(normed):
        copies[place].wait()
        total += head_product(block[...], weight[place])
    total_ref[...] = total
    copies[-1].wait()


def finish_kernel(total_ref, weight_ref, normed_ref, out_ref):
    out_ref[...] = (total_ref[...] + head_product(normed_ref[...], weight_ref[...])).astype(BF16)


def head_gather(block, axis, size):
    def shift(value, by):
        moves = [(c * size + i, c * size + (i + by * (1 - 2 * c)) % size) for c in range(2) for i in range(size)]
        return lax.ppermute(value, ("c", axis), moves)

    gathered = [(0, block)]
    if size == 8:
        far, back = shift(block, 2), shift(block, -2)
        near, behind = shift(block, 1), shift(block, -1)
        gathered += [(-1, near), (1, behind), (-2, far), (2, back)]
        gathered += [(-3, shift(far, 1)), (3, shift(back, -1))]
        opposite = shift(far, 2)
    else:
        right = block
        if size == 4:
            right, left = shift(block, 1), shift(block, -1)
            gathered += [(-1, right), (1, left)]
        opposite = shift(right, 1)
    return gathered, opposite


def local(sizes, queries, key_rows, value_rows, input_gate, forget_gate, norm_gain, output_gate, out_weight):
    planes, columns, cores, heads = sizes
    chips = planes * columns
    length, key_width = queries.shape
    value_width = value_rows.shape[1]
    core = lax.axis_index("c")
    head = lax.axis_index("y")
    chip = lax.axis_index(("z", "x"))
    count = key_width * value_width // (TILE[0] * TILE[1])
    per = count // 2 // chips

    offsets = (heads // 2 - 1, heads // 2)
    shards = [
        lax.ppermute(
            out_weight.T,
            ("z", "y"),
            [
                (z * heads + h, (h + offset) % heads * heads + z)
                for z in range(planes)
                for h in range(heads)
            ],
        )
        for offset in offsets
    ]
    tile_array = functools.partial(jax.ShapeDtypeStruct, dtype=BF16)
    state_tiles, rows = call(
        front_kernel,
        (tile_array((count + 1, *TILE)), jax.ShapeDtypeStruct((16, length), F32)),
        "hhhh",
        [
            pltpu.VMEM(key_rows.shape, BF16),
            pltpu.VMEM(value_rows.shape, BF16),
            pltpu.VMEM(input_gate.shape, F32),
            pltpu.VMEM(forget_gate.shape, F32),
            pltpu.SemaphoreType.DMA((4,)),
        ],
        vmem=60,
    )(key_rows, value_rows, input_gate, forget_gate)
    both = lax.all_gather(state_tiles, "c")
    send = call(pair_kernel, tile_array((chips, per * TILE[0] + 8, TILE[1])), "sv")(core[None], both)
    shards, send = lax.optimization_barrier((shards, send))
    groups = [
        [(z * columns + x) * cores + c for z in range(first, planes, 2) for x in range(columns) for c in range(cores)]
        for first in range(2)
    ]
    weight = lax.all_gather(jnp.concatenate(shards, axis=0), ("z", "x", "c"), axis_index_groups=groups)
    weight = weight.reshape(planes // 2, columns * cores, 2, *out_weight.shape[::-1])

    held = lax.all_to_all(send, ("z", "x"), 0, 0, tiled=True)
    intra, query_held, stats = call(
        block_kernel,
        (
            jax.ShapeDtypeStruct(value_rows.shape, F32),
            jax.ShapeDtypeStruct(queries.shape, BF16),
            jax.ShapeDtypeStruct((length, 128), F32),
        ),
        "hhhv",
        [
            pltpu.VMEM(key_rows.shape, BF16),
            pltpu.VMEM(value_rows.shape, BF16),
            pltpu.SemaphoreType.DMA((3,)),
        ],
        flops=2 * length * length * (key_width + value_width),
    )(queries, key_rows, value_rows, rows)
    held, intra = lax.optimization_barrier((held, intra))
    starts, start_max = call(
        prefix_kernel,
        (tile_array((chips, per * TILE[0], TILE[1])), jax.ShapeDtypeStruct((8, TILE[1]), F32)),
        "sv",
        [pltpu.VMEM((chips, 8, TILE[1]), F32)],
    )(chip[None], held)
    back = lax.all_to_all(starts, ("z", "x"), 0, 0, tiled=True)
    gates = call(gate_kernel, jax.ShapeDtypeStruct(value_rows.shape, F32), "vv", moved=2**20)(
        norm_gain[None], output_gate
    )
    back, gates = lax.optimization_barrier((back, gates))
    start_tiles = lax.all_gather(back, "c").reshape(count, *TILE)
    normed = call(
        memory_kernel,
        tile_array((length, value_width)),
        "svvvvvvv",
        [pltpu.VMEM((key_width, value_width), BF16)],
    )(core[None], intra, query_held, gates, stats, start_tiles, both, start_max)
    gathered, opposite = head_gather(normed, "y", heads)
    parity = lax.axis_index("z") % 2
    way = 1 - 2 * core
    where = []
    for place in [place for place, _ in gathered] + [heads // 2]:
        owners = [(head + way * place + offset) % heads for offset in offsets]
        part = (owners[0] % 2 != parity).astype(jnp.int32)
        where += [jnp.where(part == 0, owners[0], owners[1]) // 2, part]
    total, last = call(
        project_kernel,
        (
            jax.ShapeDtypeStruct((length, value_width), F32),
            tile_array((columns * cores, *weight.shape[3:])),
        ),
        "sh" + "v" * len(gathered),
        [
            pltpu.VMEM((len(gathered), columns * cores, *weight.shape[3:]), BF16),
            pltpu.SemaphoreType.DMA((len(gathered) + 1,)),
        ],
        flops=2 * length * value_width * value_width * heads,
        moved=2**23,
    )(jnp.stack(where).astype(jnp.int32), weight, *[block for _, block in gathered])
    return call(finish_kernel, tile_array((length, value_width)), "vvv")(total, last, opposite)


def solution(mesh, sizes=(8, 4, 2, 8)):
    grid = Mesh(mesh.devices.reshape(sizes), ("z", "x", "c", "y"))
    seq = ("z", "x", "c")
    in_specs = (
        P(seq, "y"), P(seq, "y"), P(seq, "y"), P("y", seq), P("y", seq), P("y"), P(seq, "y"), P("y", seq)
    )
    return jax.shard_map(
        functools.partial(local, sizes), mesh=grid, in_specs=in_specs, out_specs=P(seq, "y"), check_vma=False
    )
```

```python
import functools
import math

import jax
import jax.numpy as jnp
from jax import lax
from jax.experimental import pallas as pl
from jax.experimental.pallas import tpu as pltpu
from jax.sharding import Mesh, PartitionSpec as P

NEG = -1e30
TILE = (16, 128)
F32 = jnp.float32
BF16 = jnp.bfloat16
VMEM = pl.BlockSpec(memory_space=pltpu.VMEM)
SMEM = pl.BlockSpec(memory_space=pltpu.SMEM)
HBM = pl.BlockSpec(memory_space=pl.ANY)


def call(kernel, out_shape, places, scratch=(), flops=0, moved=2**20, vmem=48):
    return pl.pallas_call(
        kernel,
        out_shape=out_shape,
        in_specs=[{"s": SMEM, "v": VMEM, "h": HBM}[place] for place in places],
        out_specs=jax.tree.map(lambda _: VMEM, out_shape),
        scratch_shapes=list(scratch),
        compiler_params=pltpu.CompilerParams(vmem_limit_bytes=vmem * 2**20),
        cost_estimate=pl.CostEstimate(flops=flops, bytes_accessed=moved, transcendentals=0),
    )


def fetch(refs, held, semaphores):
    copies = [
        pltpu.make_async_copy(ref, buffer, semaphores.at[place])
        for place, (ref, buffer) in enumerate(zip(refs, held))
    ]
    for copy in copies:
        copy.start()
    return copies


def tiles(rows, cols):
    return [(r, c) for r in range(0, rows, TILE[0]) for c in range(0, cols, TILE[1])]


def split3(value):
    high = value.astype(BF16).astype(F32)
    middle = (value - high).astype(BF16).astype(F32)
    return high, middle, value - high - middle


def scalar_tile(end_max, decay):
    rows = lax.broadcasted_iota(jnp.int32, TILE, 0)
    held = jnp.zeros(TILE, F32)
    for place, term in enumerate(split3(end_max) + split3(decay)):
        held = jnp.where(rows == place, jnp.broadcast_to(term, TILE), held)
    return held.astype(BF16)


def scalars_of(tile):
    held = tile.astype(F32)
    end_max = held[0:1] + held[1:2] + held[2:3]
    decay = held[3:4] + held[4:5] + held[5:6]
    return end_max, decay


def front_kernel(key_hbm, value_hbm, in_hbm, forget_hbm, tiles_ref, rows_ref, keys, values, gates_in, gates, semaphores):
    copies = fetch((forget_hbm, in_hbm, key_hbm, value_hbm), (gates, gates_in, keys, values), semaphores)
    length = keys.shape[0]
    copies[0].wait()
    gate = gates[...]
    log_forget = jnp.minimum(gate, 0.0) - jnp.log1p(jnp.exp(-jnp.abs(gate)))
    log_forget = jnp.broadcast_to(log_forget, (8, length))
    before = lax.broadcasted_iota(jnp.int32, (length, length), 0)
    after = lax.broadcasted_iota(jnp.int32, (length, length), 1)
    upper = jnp.where(before <= after, 1.0, 0.0).astype(F32)
    cum = jnp.dot(log_forget, upper, precision=lax.Precision.HIGHEST, preferred_element_type=F32)
    rows_ref[0:8] = cum
    decay = cum[0:1, length - 1 : length]
    copies[1].wait()
    rows_ref[8:16] = jnp.broadcast_to(gates_in[...], (8, length))
    end_weight = decay - cum[0:1] + gates_in[...]
    end_max = jnp.max(end_weight, axis=1, keepdims=True)
    copies[2].wait()
    scaled = (keys[...].astype(F32).T * jnp.exp(end_weight - end_max)).astype(BF16)
    copies[3].wait()
    state = jnp.dot(scaled, values[...], preferred_element_type=F32).astype(BF16)
    places = tiles(*state.shape)
    for place, (row, col) in enumerate(places):
        tiles_ref[place] = state[row : row + TILE[0], col : col + TILE[1]]
    tiles_ref[len(places)] = scalar_tile(end_max, decay)


def pair_kernel(core_ref, both_ref, send_ref):
    core = core_ref[0]
    owners = send_ref.shape[0]
    last = both_ref.shape[1] - 1
    half = last // 2
    per = half // owners
    max_0, decay_0 = scalars_of(both_ref[0, last])
    max_1, decay_1 = scalars_of(both_ref[1, last])
    end_max = jnp.maximum(decay_1 + max_0, max_1)
    scale_0 = jnp.exp(decay_1 + max_0 - end_max)
    scale_1 = jnp.exp(max_1 - end_max)
    scalars = scalar_tile(end_max, decay_0 + decay_1)
    for owner in range(owners):
        for piece in range(per):
            place = core * half + owner * per + piece
            send_ref[owner, piece * 16 : piece * 16 + 16] = (
                scale_0 * both_ref[0, place].astype(F32) + scale_1 * both_ref[1, place].astype(F32)
            ).astype(BF16)
        send_ref[owner, per * 16 : per * 16 + 8] = scalars[0:8]


def prefix_kernel(chip_ref, held_ref, state_ref, max_ref, maxes):
    chips, rows, lanes = state_ref.shape
    state = jnp.zeros((rows, lanes), F32)
    start_max = jnp.full((1, lanes), NEG, F32)
    for chip in range(chips):
        state_ref[chip] = state.astype(BF16)
        maxes[chip] = jnp.broadcast_to(start_max, (8, lanes))
        end_max, decay = scalars_of(held_ref[chip, rows : rows + 8])
        new_max = jnp.maximum(decay + start_max, end_max)
        state = jnp.exp(decay + start_max - new_max) * state + jnp.exp(
            end_max - new_max
        ) * held_ref[chip, 0:rows].astype(F32)
        start_max = new_max
    max_ref[...] = maxes[chip_ref[0]]


def block_kernel(
    query_hbm, key_hbm, value_hbm, rows_ref, intra_ref, query_ref, stats_ref, keys, values, semaphores
):
    copies = fetch((query_hbm, key_hbm, value_hbm), (query_ref, keys, values), semaphores)
    length, width = query_ref.shape
    cum_row = rows_ref[0:1]
    cum_col = rows_ref[0:8].T[:, 0:1]
    at = lax.broadcasted_iota(jnp.int32, (length, length), 0)
    by = lax.broadcasted_iota(jnp.int32, (length, length), 1)
    log_weight = jnp.where(at >= by, cum_col - cum_row + rows_ref[8:9], NEG)
    local_max = jnp.max(log_weight, axis=1, keepdims=True)
    lane = lax.broadcasted_iota(jnp.int32, stats_ref.shape, 1)
    stats_ref[...] = jnp.where(lane == 0, cum_col, local_max)
    copies[0].wait()
    copies[1].wait()
    scores = lax.dot_general(
        query_ref[...], keys[...], (((1,), (1,)), ((), ())), preferred_element_type=F32
    ) * (1.0 / math.sqrt(width))
    weights = (jnp.exp(log_weight - local_max) * scores).astype(BF16)
    copies[2].wait()
    intra_ref[...] = jnp.dot(weights, values[...], preferred_element_type=F32)


def gate_kernel(gain_ref, gate_ref, out_ref):
    out_ref[...] = gain_ref[...] * jax.nn.sigmoid(gate_ref[...].astype(F32))


def memory_kernel(
    core_ref, intra_ref, query_ref, gate_ref, stats_ref, tiles_ref, both_ref, max_ref, normed_ref, state
):
    inv_root = 1.0 / math.sqrt(query_ref.shape[1])
    second = core_ref[0] == 1
    chip_max = max_ref[0:1]
    first_max, first_decay = scalars_of(both_ref[0, both_ref.shape[1] - 1])
    moved = jnp.maximum(first_decay + chip_max, first_max)
    start = jnp.where(second, moved, chip_max)
    keep = jnp.where(second, jnp.exp(first_decay + chip_max - moved), 1.0)
    add = jnp.where(second, jnp.exp(first_max - moved), 0.0)
    for place, (row, col) in enumerate(tiles(*state.shape)):
        state[row : row + TILE[0], col : col + TILE[1]] = (
            keep * tiles_ref[place].astype(F32) + add * both_ref[0, place].astype(F32)
        ).astype(BF16)
    local_max = stats_ref[:, 1:2]
    carried_weight = stats_ref[:, 0:1] + start[:, 0:1]
    row_max = jnp.maximum(carried_weight, local_max)
    carried = jnp.dot(query_ref[...], state[...], preferred_element_type=F32)
    memory = (
        jnp.exp(local_max - row_max) * intra_ref[...]
        + (jnp.exp(carried_weight - row_max) * inv_root) * carried
    )
    centred = memory - jnp.mean(memory, axis=1, keepdims=True)
    spread = jnp.mean(centred * centred, axis=1, keepdims=True)
    normed_ref[...] = (centred * lax.rsqrt(spread + 1e-06) * gate_ref[...]).astype(BF16)


def head_product(normed, weight):
    rows = weight.reshape(-1, weight.shape[-1])
    return lax.dot_general(normed, rows, (((1,), (1,)), ((), ())), preferred_element_type=F32)


def project_kernel(where_ref, weight_hbm, *refs):
    normed, (total_ref, last_ref, weight, semaphores) = refs[:-4], refs[-4:]
    copies = [
        pltpu.make_async_copy(
            weight_hbm.at[where_ref[2 * place], :, where_ref[2 * place + 1]],
            weight.at[place] if place < len(normed) else last_ref,
            semaphores.at[place],
        )
        for place in range(len(normed) + 1)
    ]
    for copy in copies:
        copy.start()
    total = jnp.zeros(total_ref.shape, F32)
    for place, block in enumerate(normed):
        copies[place].wait()
        total += head_product(block[...], weight[place])
    total_ref[...] = total
    copies[-1].wait()


def finish_kernel(total_ref, weight_ref, normed_ref, out_ref):
    out_ref[...] = (total_ref[...] + head_product(normed_ref[...], weight_ref[...])).astype(BF16)


def head_gather(block, axis, size):
    def shift(value, by):
        moves = [(c * size + i, c * size + (i + by * (1 - 2 * c)) % size) for c in range(2) for i in range(size)]
        return lax.ppermute(value, ("c", axis), moves)

    gathered = [(0, block)]
    if size == 8:
        far, back = shift(block, 2), shift(block, -2)
        near, behind = shift(block, 1), shift(block, -1)
        gathered += [(-1, near), (1, behind), (-2, far), (2, back)]
        gathered += [(-3, shift(far, 1)), (3, shift(back, -1))]
        opposite = shift(far, 2)
    else:
        right = block
        if size == 4:
            right, left = shift(block, 1), shift(block, -1)
            gathered += [(-1, right), (1, left)]
        opposite = shift(right, 1)
    return gathered, opposite


def local(sizes, queries, key_rows, value_rows, input_gate, forget_gate, norm_gain, output_gate, out_weight):
    planes, columns, cores, heads = sizes
    chips = planes * columns
    length, key_width = queries.shape
    value_width = value_rows.shape[1]
    core = lax.axis_index("c")
    head = lax.axis_index("y")
    chip = lax.axis_index(("z", "x"))
    count = key_width * value_width // (TILE[0] * TILE[1])
    per = count // 2 // chips

    offsets = (heads // 2 - 1, heads // 2)
    shards = [
        lax.ppermute(
            out_weight.T,
            ("z", "c", "y"),
            [
                ((z * cores + c) * heads + h, ((h + offsets[turn ^ c]) % heads * cores + c) * heads + z)
                for z in range(planes)
                for c in range(cores)
                for h in range(heads)
            ],
        )
        for turn in range(2)
    ]
    tile_array = functools.partial(jax.ShapeDtypeStruct, dtype=BF16)
    state_tiles, rows = call(
        front_kernel,
        (tile_array((count + 1, *TILE)), jax.ShapeDtypeStruct((16, length), F32)),
        "hhhh",
        [
            pltpu.VMEM(key_rows.shape, BF16),
            pltpu.VMEM(value_rows.shape, BF16),
            pltpu.VMEM(input_gate.shape, F32),
            pltpu.VMEM(forget_gate.shape, F32),
            pltpu.SemaphoreType.DMA((4,)),
        ],
        vmem=60,
    )(key_rows, value_rows, input_gate, forget_gate)
    both = lax.all_gather(state_tiles, "c")
    send = call(pair_kernel, tile_array((chips, per * TILE[0] + 8, TILE[1])), "sv")(core[None], both)
    shards, send = lax.optimization_barrier((shards, send))
    groups = [
        [(z * columns + x) * cores + c for z in range(first, planes, 2) for x in range(columns) for c in range(cores)]
        for first in range(2)
    ]
    first, second = shards
    shards = [jnp.where(core == 0, first, second), jnp.where(core == 0, second, first)]
    weight = lax.all_gather(jnp.concatenate(shards, axis=0), ("z", "x", "c"), axis_index_groups=groups)
    weight = weight.reshape(planes // 2, columns * cores, 2, *out_weight.shape[::-1])

    held = lax.all_to_all(send, ("z", "x"), 0, 0, tiled=True)
    intra, query_held, stats = call(
        block_kernel,
        (
            jax.ShapeDtypeStruct(value_rows.shape, F32),
            jax.ShapeDtypeStruct(queries.shape, BF16),
            jax.ShapeDtypeStruct((length, 128), F32),
        ),
        "hhhv",
        [
            pltpu.VMEM(key_rows.shape, BF16),
            pltpu.VMEM(value_rows.shape, BF16),
            pltpu.SemaphoreType.DMA((3,)),
        ],
        flops=2 * length * length * (key_width + value_width),
    )(queries, key_rows, value_rows, rows)
    held, intra = lax.optimization_barrier((held, intra))
    starts, start_max = call(
        prefix_kernel,
        (tile_array((chips, per * TILE[0], TILE[1])), jax.ShapeDtypeStruct((8, TILE[1]), F32)),
        "sv",
        [pltpu.VMEM((chips, 8, TILE[1]), F32)],
    )(chip[None], held)
    back = lax.all_to_all(starts, ("z", "x"), 0, 0, tiled=True)
    gates = call(gate_kernel, jax.ShapeDtypeStruct(value_rows.shape, F32), "vv", moved=2**20)(
        norm_gain[None], output_gate
    )
    back, gates = lax.optimization_barrier((back, gates))
    start_tiles = lax.all_gather(back, "c").reshape(count, *TILE)
    normed = call(
        memory_kernel,
        tile_array((length, value_width)),
        "svvvvvvv",
        [pltpu.VMEM((key_width, value_width), BF16)],
    )(core[None], intra, query_held, gates, stats, start_tiles, both, start_max)
    gathered, opposite = head_gather(normed, "y", heads)
    parity = lax.axis_index("z") % 2
    way = 1 - 2 * core
    where = []
    for place in [place for place, _ in gathered] + [heads // 2]:
        owners = [(head + way * place + offset) % heads for offset in offsets]
        part = (owners[0] % 2 != parity).astype(jnp.int32)
        where += [jnp.where(part == 0, owners[0], owners[1]) // 2, part]
    total, last = call(
        project_kernel,
        (
            jax.ShapeDtypeStruct((length, value_width), F32),
            tile_array((columns * cores, *weight.shape[3:])),
        ),
        "sh" + "v" * len(gathered),
        [
            pltpu.VMEM((len(gathered), columns * cores, *weight.shape[3:]), BF16),
            pltpu.SemaphoreType.DMA((len(gathered) + 1,)),
        ],
        flops=2 * length * value_width * value_width * heads,
        moved=2**23,
    )(jnp.stack(where).astype(jnp.int32), weight, *[block for _, block in gathered])
    return call(finish_kernel, tile_array((length, value_width)), "vvv")(total, last, opposite)


def solution(mesh, sizes=(8, 4, 2, 8)):
    grid = Mesh(mesh.devices.reshape(sizes), ("z", "x", "c", "y"))
    seq = ("z", "x", "c")
    in_specs = (
        P(seq, "y"), P(seq, "y"), P(seq, "y"), P("y", seq), P("y", seq), P("y"), P(seq, "y"), P("y", seq)
    )
    return jax.shard_map(
        functools.partial(local, sizes), mesh=grid, in_specs=in_specs, out_specs=P(seq, "y"), check_vma=False
    )
```

```python
import functools
import math

import jax
import jax.numpy as jnp
from jax import lax
from jax.experimental import pallas as pl
from jax.experimental.pallas import tpu as pltpu
from jax.sharding import Mesh, PartitionSpec as P

NEG = -1e30
TILE = (16, 128)
F32 = jnp.float32
BF16 = jnp.bfloat16
VMEM = pl.BlockSpec(memory_space=pltpu.VMEM)
SMEM = pl.BlockSpec(memory_space=pltpu.SMEM)
HBM = pl.BlockSpec(memory_space=pl.ANY)


def call(kernel, out_shape, places, scratch=(), flops=0, moved=2**20, vmem=48):
    return pl.pallas_call(
        kernel,
        out_shape=out_shape,
        in_specs=[{"s": SMEM, "v": VMEM, "h": HBM}[place] for place in places],
        out_specs=jax.tree.map(lambda _: VMEM, out_shape),
        scratch_shapes=list(scratch),
        compiler_params=pltpu.CompilerParams(vmem_limit_bytes=vmem * 2**20),
        cost_estimate=pl.CostEstimate(flops=flops, bytes_accessed=moved, transcendentals=0),
    )


def fetch(refs, held, semaphores):
    copies = [
        pltpu.make_async_copy(ref, buffer, semaphores.at[place])
        for place, (ref, buffer) in enumerate(zip(refs, held))
    ]
    for copy in copies:
        copy.start()
    return copies


def tiles(rows, cols):
    return [(r, c) for r in range(0, rows, TILE[0]) for c in range(0, cols, TILE[1])]


def split3(value):
    high = value.astype(BF16).astype(F32)
    middle = (value - high).astype(BF16).astype(F32)
    return high, middle, value - high - middle


def scalar_tile(end_max, decay):
    rows = lax.broadcasted_iota(jnp.int32, TILE, 0)
    held = jnp.zeros(TILE, F32)
    for place, term in enumerate(split3(end_max) + split3(decay)):
        held = jnp.where(rows == place, jnp.broadcast_to(term, TILE), held)
    return held.astype(BF16)


def scalars_of(tile):
    held = tile.astype(F32)
    end_max = held[0:1] + held[1:2] + held[2:3]
    decay = held[3:4] + held[4:5] + held[5:6]
    return end_max, decay


def front_kernel(key_hbm, value_hbm, in_hbm, forget_hbm, tiles_ref, rows_ref, keys, values, gates_in, gates, semaphores):
    copies = fetch((forget_hbm, in_hbm, key_hbm, value_hbm), (gates, gates_in, keys, values), semaphores)
    length = keys.shape[0]
    copies[0].wait()
    gate = gates[...]
    log_forget = jnp.minimum(gate, 0.0) - jnp.log1p(jnp.exp(-jnp.abs(gate)))
    log_forget = jnp.broadcast_to(log_forget, (8, length))
    before = lax.broadcasted_iota(jnp.int32, (length, length), 0)
    after = lax.broadcasted_iota(jnp.int32, (length, length), 1)
    upper = jnp.where(before <= after, 1.0, 0.0).astype(F32)
    cum = jnp.dot(log_forget, upper, precision=lax.Precision.HIGHEST, preferred_element_type=F32)
    rows_ref[0:8] = cum
    decay = cum[0:1, length - 1 : length]
    copies[1].wait()
    rows_ref[8:16] = jnp.broadcast_to(gates_in[...], (8, length))
    end_weight = decay - cum[0:1] + gates_in[...]
    end_max = jnp.max(end_weight, axis=1, keepdims=True)
    copies[2].wait()
    scaled = (keys[...].astype(F32).T * jnp.exp(end_weight - end_max)).astype(BF16)
    copies[3].wait()
    state = jnp.dot(scaled, values[...], preferred_element_type=F32).astype(BF16)
    places = tiles(*state.shape)
    for place, (row, col) in enumerate(places):
        tiles_ref[place] = state[row : row + TILE[0], col : col + TILE[1]]
    tiles_ref[len(places)] = scalar_tile(end_max, decay)


def pair_kernel(core_ref, both_ref, send_ref):
    core = core_ref[0]
    owners = send_ref.shape[0]
    last = both_ref.shape[1] - 1
    half = last // 2
    per = half // owners
    max_0, decay_0 = scalars_of(both_ref[0, last])
    max_1, decay_1 = scalars_of(both_ref[1, last])
    end_max = jnp.maximum(decay_1 + max_0, max_1)
    scale_0 = jnp.exp(decay_1 + max_0 - end_max)
    scale_1 = jnp.exp(max_1 - end_max)
    scalars = scalar_tile(end_max, decay_0 + decay_1)
    for owner in range(owners):
        for piece in range(per):
            place = core * half + owner * per + piece
            send_ref[owner, piece * 16 : piece * 16 + 16] = (
                scale_0 * both_ref[0, place].astype(F32) + scale_1 * both_ref[1, place].astype(F32)
            ).astype(BF16)
        send_ref[owner, per * 16 : per * 16 + 8] = scalars[0:8]


def prefix_kernel(chip_ref, held_ref, state_ref, max_ref, maxes):
    chips, rows, lanes = state_ref.shape
    state = jnp.zeros((rows, lanes), F32)
    start_max = jnp.full((1, lanes), NEG, F32)
    for chip in range(chips):
        state_ref[chip] = state.astype(BF16)
        maxes[chip] = jnp.broadcast_to(start_max, (8, lanes))
        end_max, decay = scalars_of(held_ref[chip, rows : rows + 8])
        new_max = jnp.maximum(decay + start_max, end_max)
        state = jnp.exp(decay + start_max - new_max) * state + jnp.exp(
            end_max - new_max
        ) * held_ref[chip, 0:rows].astype(F32)
        start_max = new_max
    max_ref[...] = maxes[chip_ref[0]]


def block_kernel(
    query_hbm, key_hbm, value_hbm, rows_ref, intra_ref, query_ref, stats_ref, keys, values, semaphores
):
    copies = fetch((query_hbm, key_hbm, value_hbm), (query_ref, keys, values), semaphores)
    length, width = query_ref.shape
    cum_row = rows_ref[0:1]
    cum_col = rows_ref[0:8].T[:, 0:1]
    at = lax.broadcasted_iota(jnp.int32, (length, length), 0)
    by = lax.broadcasted_iota(jnp.int32, (length, length), 1)
    log_weight = jnp.where(at >= by, cum_col - cum_row + rows_ref[8:9], NEG)
    local_max = jnp.max(log_weight, axis=1, keepdims=True)
    lane = lax.broadcasted_iota(jnp.int32, stats_ref.shape, 1)
    stats_ref[...] = jnp.where(lane == 0, cum_col, local_max)
    copies[0].wait()
    copies[1].wait()
    scores = lax.dot_general(
        query_ref[...], keys[...], (((1,), (1,)), ((), ())), preferred_element_type=F32
    ) * (1.0 / math.sqrt(width))
    weights = (jnp.exp(log_weight - local_max) * scores).astype(BF16)
    copies[2].wait()
    intra_ref[...] = jnp.dot(weights, values[...], preferred_element_type=F32)


def gate_kernel(gain_ref, gate_ref, out_ref):
    out_ref[...] = gain_ref[...] * jax.nn.sigmoid(gate_ref[...].astype(F32))


def memory_kernel(
    core_ref, intra_ref, query_ref, gate_ref, stats_ref, tiles_ref, both_ref, max_ref, normed_ref, state
):
    inv_root = 1.0 / math.sqrt(query_ref.shape[1])
    second = core_ref[0] == 1
    chip_max = max_ref[0:1]
    first_max, first_decay = scalars_of(both_ref[0, both_ref.shape[1] - 1])
    moved = jnp.maximum(first_decay + chip_max, first_max)
    start = jnp.where(second, moved, chip_max)
    keep = jnp.where(second, jnp.exp(first_decay + chip_max - moved), 1.0)
    add = jnp.where(second, jnp.exp(first_max - moved), 0.0)
    for place, (row, col) in enumerate(tiles(*state.shape)):
        state[row : row + TILE[0], col : col + TILE[1]] = (
            keep * tiles_ref[place].astype(F32) + add * both_ref[0, place].astype(F32)
        ).astype(BF16)
    local_max = stats_ref[:, 1:2]
    carried_weight = stats_ref[:, 0:1] + start[:, 0:1]
    row_max = jnp.maximum(carried_weight, local_max)
    carried = jnp.dot(query_ref[...], state[...], preferred_element_type=F32)
    memory = (
        jnp.exp(local_max - row_max) * intra_ref[...]
        + (jnp.exp(carried_weight - row_max) * inv_root) * carried
    )
    centred = memory - jnp.mean(memory, axis=1, keepdims=True)
    spread = jnp.mean(centred * centred, axis=1, keepdims=True)
    normed_ref[...] = (centred * lax.rsqrt(spread + 1e-06) * gate_ref[...]).astype(BF16)


def head_product(normed, weight):
    rows = weight.reshape(-1, weight.shape[-1])
    return lax.dot_general(normed, rows, (((1,), (1,)), ((), ())), preferred_element_type=F32)


def project_kernel(where_ref, weight_hbm, *refs):
    normed, (total_ref, last_ref, weight, semaphores) = refs[:-4], refs[-4:]
    copies = [
        pltpu.make_async_copy(
            weight_hbm.at[where_ref[2 * place], :, where_ref[2 * place + 1]],
            weight.at[place] if place < len(normed) else last_ref,
            semaphores.at[place],
        )
        for place in range(len(normed) + 1)
    ]
    for copy in copies:
        copy.start()
    total = jnp.zeros(total_ref.shape, F32)
    for place, block in enumerate(normed):
        copies[place].wait()
        total += head_product(block[...], weight[place])
    total_ref[...] = total
    copies[-1].wait()


def finish_kernel(total_ref, weight_ref, normed_ref, out_ref):
    out_ref[...] = (total_ref[...] + head_product(normed_ref[...], weight_ref[...])).astype(BF16)


def head_gather(block, axis, size):
    def shift(value, by):
        moves = [(c * size + i, c * size + (i + by * (1 - 2 * c)) % size) for c in range(2) for i in range(size)]
        return lax.ppermute(value, ("c", axis), moves)

    gathered = [(0, block)]
    if size == 8:
        far, back = shift(block, 2), shift(block, -2)
        near, behind = shift(block, 1), shift(block, -1)
        gathered += [(-1, near), (1, behind), (-2, far), (2, back)]
        gathered += [(-3, shift(far, 1)), (3, shift(back, -1))]
        opposite = shift(back, -2)
    else:
        right = block
        if size == 4:
            right, left = shift(block, 1), shift(block, -1)
            gathered += [(-1, right), (1, left)]
        opposite = shift(right, 1)
    return gathered, opposite


def local(sizes, queries, key_rows, value_rows, input_gate, forget_gate, norm_gain, output_gate, out_weight):
    planes, columns, cores, heads = sizes
    chips = planes * columns
    length, key_width = queries.shape
    value_width = value_rows.shape[1]
    core = lax.axis_index("c")
    head = lax.axis_index("y")
    chip = lax.axis_index(("z", "x"))
    count = key_width * value_width // (TILE[0] * TILE[1])
    per = count // 2 // chips

    offsets = (heads // 2 - 1, heads // 2 - 2)
    shards = [
        lax.ppermute(
            out_weight.T,
            ("z", "y"),
            [
                (z * heads + h, (h + offset) % heads * heads + z)
                for z in range(planes)
                for h in range(heads)
            ],
        )
        for offset in offsets
    ]
    tile_array = functools.partial(jax.ShapeDtypeStruct, dtype=BF16)
    state_tiles, rows = call(
        front_kernel,
        (tile_array((count + 1, *TILE)), jax.ShapeDtypeStruct((16, length), F32)),
        "hhhh",
        [
            pltpu.VMEM(key_rows.shape, BF16),
            pltpu.VMEM(value_rows.shape, BF16),
            pltpu.VMEM(input_gate.shape, F32),
            pltpu.VMEM(forget_gate.shape, F32),
            pltpu.SemaphoreType.DMA((4,)),
        ],
        vmem=60,
    )(key_rows, value_rows, input_gate, forget_gate)
    both = lax.all_gather(state_tiles, "c")
    send = call(pair_kernel, tile_array((chips, per * TILE[0] + 8, TILE[1])), "sv")(core[None], both)
    shards, send = lax.optimization_barrier((shards, send))
    groups = [
        [(z * columns + x) * cores + c for z in range(first, planes, 2) for x in range(columns) for c in range(cores)]
        for first in range(2)
    ]
    weight = lax.all_gather(jnp.concatenate(shards, axis=0), ("z", "x", "c"), axis_index_groups=groups)
    weight = weight.reshape(planes // 2, columns * cores, 2, *out_weight.shape[::-1])

    held = lax.all_to_all(send, ("z", "x"), 0, 0, tiled=True)
    intra, query_held, stats = call(
        block_kernel,
        (
            jax.ShapeDtypeStruct(value_rows.shape, F32),
            jax.ShapeDtypeStruct(queries.shape, BF16),
            jax.ShapeDtypeStruct((length, 128), F32),
        ),
        "hhhv",
        [
            pltpu.VMEM(key_rows.shape, BF16),
            pltpu.VMEM(value_rows.shape, BF16),
            pltpu.SemaphoreType.DMA((3,)),
        ],
        flops=2 * length * length * (key_width + value_width),
    )(queries, key_rows, value_rows, rows)
    held, intra = lax.optimization_barrier((held, intra))
    starts, start_max = call(
        prefix_kernel,
        (tile_array((chips, per * TILE[0], TILE[1])), jax.ShapeDtypeStruct((8, TILE[1]), F32)),
        "sv",
        [pltpu.VMEM((chips, 8, TILE[1]), F32)],
    )(chip[None], held)
    back = lax.all_to_all(starts, ("z", "x"), 0, 0, tiled=True)
    gates = call(gate_kernel, jax.ShapeDtypeStruct(value_rows.shape, F32), "vv", moved=2**20)(
        norm_gain[None], output_gate
    )
    back, gates = lax.optimization_barrier((back, gates))
    start_tiles = lax.all_gather(back, "c").reshape(count, *TILE)
    normed = call(
        memory_kernel,
        tile_array((length, value_width)),
        "svvvvvvv",
        [pltpu.VMEM((key_width, value_width), BF16)],
    )(core[None], intra, query_held, gates, stats, start_tiles, both, start_max)
    gathered, opposite = head_gather(normed, "y", heads)
    parity = lax.axis_index("z") % 2
    way = 1 - 2 * core
    where = []
    for place in [place for place, _ in gathered] + [heads // 2]:
        owners = [(head + way * place + offset) % heads for offset in offsets]
        part = (owners[0] % 2 != parity).astype(jnp.int32)
        where += [jnp.where(part == 0, owners[0], owners[1]) // 2, part]
    total, last = call(
        project_kernel,
        (
            jax.ShapeDtypeStruct((length, value_width), F32),
            tile_array((columns * cores, *weight.shape[3:])),
        ),
        "sh" + "v" * len(gathered),
        [
            pltpu.VMEM((len(gathered), columns * cores, *weight.shape[3:]), BF16),
            pltpu.SemaphoreType.DMA((len(gathered) + 1,)),
        ],
        flops=2 * length * value_width * value_width * heads,
        moved=2**23,
    )(jnp.stack(where).astype(jnp.int32), weight, *[block for _, block in gathered])
    return call(finish_kernel, tile_array((length, value_width)), "vvv")(total, last, opposite)


def solution(mesh, sizes=(8, 4, 2, 8)):
    grid = Mesh(mesh.devices.reshape(sizes), ("z", "x", "c", "y"))
    seq = ("z", "x", "c")
    in_specs = (
        P(seq, "y"), P(seq, "y"), P(seq, "y"), P("y", seq), P("y", seq), P("y"), P(seq, "y"), P("y", seq)
    )
    return jax.shard_map(
        functools.partial(local, sizes), mesh=grid, in_specs=in_specs, out_specs=P(seq, "y"), check_vma=False
    )
```
